32 devices in a mesh: layer: 4 (over y, core), unit: 8 (over z, x).
Axes of the slice: x: 2, y: 2, z: 4, core: 2. Of those that a mesh axis runs over, the one named last changes fastest.
Arguments:
- tokens: int32 [4, 32], replicated, may hold values from 0 to 255
- embed: bfloat16 [256, 8192], P(None, 'unit'), may hold values from -6 to 6
- weights: bfloat16 [4, 128, 32, 64, 256], P('layer', 'unit'), may hold values from -0.125 to 0.125
- layout: int32 [4, 128, 32], P('layer', 'unit'), may hold values from 0 to 255, as said below
- bias: float32 [4, 128, 256], P('layer', 'unit'), may hold values from -4 to 4
- d_hidden: bfloat16 [4, 4, 32, 8192], P('layer', None, None, 'unit'), may hold values from -6 to 6
Outputs:
- hidden: bfloat16 [4, 4, 32, 8192], P('layer', None, None, 'unit')
- grad_weights: bfloat16 [4, 128, 32, 64, 256], P('layer', 'unit')
- grad_bias: float32 [4, 128, 256], P('layer', 'unit')
The draws below stay inside these ranges and needn't reach their ends.
Inputs may be any that keep to these rules, and one draw needn't show every extreme that they name: The 32 entries of every row layout[l, j] are distinct and rising; numbers under 128 are blocks of the layer's input, the others of its own previous hidden state.
All inputs are finite; a program needn't handle non-finite values.
Results may differ from the reference program's by a relative error of at most 0.0085.
Values may be sent and summed in bfloat16 or wider, within the bound.
A program may use at most 128 MiB of HBM per device.

```python
import jax
import jax.numpy as jnp
from jax import lax

H = 8192
BLK = 64
VOCAB = 256
B = 32
STEPS = 4
HB = 128
NNZ = 32
LAYERS = 4
N_UNIT = 8


def draw_layout(key, part):
    scores = jax.random.randint(key, (LAYERS, HB, 2 * HB), 0, 1 << 20) * (2 * HB) + jnp.arange(2 * HB, dtype=jnp.int32)
    chosen = lax.top_k(scores, NNZ)[1]
    return jnp.sort(chosen, axis=-1).astype(jnp.int32)


def place_ends(array, stream_key, low, top_value):
    extent = array.shape
    spot = [jax.random.randint(jax.random.fold_in(stream_key, axis), (), 0, extent[axis]) for axis in range(len(extent))]
    array = array.at[tuple(spot)].set(low)
    longest = extent.index(max(extent))
    spot[longest] = (spot[longest] + 1) % extent[longest]
    return array.at[tuple(spot)].set(top_value)


def steps_of(key, extent, split, smallest, largest):
    def one(position, blocks):
        draws = jax.random.uniform(jax.random.fold_in(jax.random.fold_in(key, 6), position), (blocks,), jnp.float32, smallest / len(split), largest / len(split))
        return jnp.repeat(jnp.exp(draws), extent[position] // blocks).reshape((-1,) + (1,) * (len(extent) - position - 1))

    gain = one(*split[0])
    for cut in split[1:]:
        gain = gain * one(*cut)
    return gain


def scatter_about(rng, shape, scale, bound, pieces=(), kind=jnp.bfloat16):
    level = steps_of(rng, shape, pieces, -0.22, 0.18) if pieces else 1.0
    values = jax.random.normal(rng, shape, jnp.float32) * scale * level
    return jnp.minimum(jnp.maximum(values, -bound), bound).astype(kind)


def setup_inputs(seed: int = 0) -> dict:
    arg_keys = jax.random.split(jax.random.key(seed), 7)
    return {
        "tokens": place_ends(jax.random.randint(arg_keys[0], (STEPS, B), 0, VOCAB), jax.random.fold_in(arg_keys[0], 1), 0, VOCAB - 1).astype(jnp.int32),
        "embed": scatter_about(arg_keys[1], (VOCAB, H), 1.0, 6.0, ((1, 8),)),
        "weights": scatter_about(arg_keys[2], (LAYERS, HB, NNZ, BLK, 4 * BLK), (NNZ * BLK) ** -0.5, 0.125, ((0, 4), (1, 8))),
        "layout": draw_layout(jax.random.fold_in(arg_keys[6], 71), 0),
        "bias": scatter_about(arg_keys[4], (LAYERS, HB, 4 * BLK), 1.0, 4.0, ((0, 4), (1, 8)), jnp.float32),
        "d_hidden": scatter_about(arg_keys[5], (LAYERS, STEPS, B, H), 1.0, 6.0, ((0, 4), (3, 8))),
    }


def gate_math(pre_act, cell_prev):
    gate_size = pre_act.shape[-1] // 4
    in_gate = jax.nn.sigmoid(pre_act[..., :gate_size])
    forget = jax.nn.sigmoid(pre_act[..., gate_size:2 * gate_size])
    update = jnp.tanh(pre_act[..., 2 * gate_size:3 * gate_size])
    out_gate = jax.nn.sigmoid(pre_act[..., 3 * gate_size:])
    cell_state = forget * cell_prev + in_gate * update
    new_hidden = (out_gate * jnp.tanh(cell_state)).astype(jnp.bfloat16)
    return jnp.concatenate([in_gate, forget, update, out_gate], -1), cell_state, new_hidden


def gate_grads(gate_acts, cell_state, cell_prev, grad_hidden, grad_carry):
    gate_size = gate_acts.shape[-1] // 4
    in_gate = gate_acts[..., :gate_size]
    forget = gate_acts[..., gate_size:2 * gate_size]
    update = gate_acts[..., 2 * gate_size:3 * gate_size]
    out_gate = gate_acts[..., 3 * gate_size:]
    squash = jnp.tanh(cell_state)
    grad_cell = grad_carry + grad_hidden * out_gate * (1.0 - squash * squash)
    grad_in = grad_cell * update * in_gate * (1.0 - in_gate)
    grad_forget = grad_cell * cell_prev * forget * (1.0 - forget)
    grad_update = grad_cell * in_gate * (1.0 - update * update)
    grad_out = grad_hidden * squash * out_gate * (1.0 - out_gate)
    grad_pre = jnp.concatenate([grad_in, grad_forget, grad_update, grad_out], -1).astype(jnp.bfloat16)
    return grad_pre, grad_cell * forget


def sparse_product(inputs, weight_f, layout_rows):
    picked = jnp.take(inputs, layout_rows, axis=1).astype(jnp.float32)
    return jnp.einsum("bjkc,jkcd->bjd", picked, weight_f)


def spread(grad_pre, weight_f, layout_rows):
    batch_rows = grad_pre.shape[0]
    group_size = HB // N_UNIT
    contrib = jnp.einsum("bjd,jkcd->bjkc", grad_pre.astype(jnp.float32), weight_f)
    contrib = contrib.reshape(batch_rows, N_UNIT, group_size * NNZ, BLK)
    index_rows = layout_rows.reshape(N_UNIT, group_size * NNZ)

    def one_group(piece, index_row):
        return jnp.zeros((batch_rows, 2 * HB, BLK), jnp.float32).at[:, index_row].add(piece)

    parts = jax.vmap(one_group, in_axes=(1, 0))(contrib, index_rows)
    rounded = lax.optimization_barrier(parts.astype(jnp.bfloat16)).astype(jnp.float32)
    return jnp.sum(rounded, 0).reshape(batch_rows, 2 * H)


def reference(tokens, embed, weights, layout, bias, d_hidden):
    source = jnp.take(embed, tokens, axis=0)
    saved = []
    hidden_all = []
    for layer_idx in range(LAYERS):
        weight_f = weights[layer_idx].astype(jnp.float32)
        layout_rows = layout[layer_idx]
        bias_rows = bias[layer_idx]

        def advance(loop_state, source_row):
            hidden_prev, cell_prev = loop_state
            inputs = jnp.concatenate([source_row, hidden_prev], -1).reshape(B, 2 * HB, BLK)
            pre_act = sparse_product(inputs, weight_f, layout_rows) + bias_rows
            gate_acts, cell_state, new_hidden = gate_math(pre_act, cell_prev)
            new_hidden = new_hidden.reshape(B, H)
            return (new_hidden, cell_state), (new_hidden, cell_state, gate_acts, inputs)

        start = (jnp.zeros((B, H), jnp.bfloat16), jnp.zeros((B, HB, BLK), jnp.float32))
        _, (hidden_seq, cell_seq, act_seq, input_seq) = lax.scan(advance, start, source)
        saved.append((cell_seq, act_seq, input_seq))
        hidden_all.append(hidden_seq)
        source = hidden_seq
    from_above = jnp.zeros((STEPS, B, H), jnp.float32)
    grad_w_all = [None] * LAYERS
    grad_b_all = [None] * LAYERS
    for layer_idx in reversed(range(LAYERS)):
        weight_f = weights[layer_idx].astype(jnp.float32)
        layout_rows = layout[layer_idx]
        cell_seq, act_seq, input_seq = saved[layer_idx]
        prev_seq = jnp.concatenate([jnp.zeros((1, B, HB, BLK), jnp.float32), cell_seq[:-1]], 0)

        def retreat(loop_state, row_items):
            grad_recur, grad_carry = loop_state
            upstream, above, gate_acts, cell_state, cell_prev = row_items
            grad_hidden = upstream.astype(jnp.float32) + above + grad_recur
            grad_pre, carry_new = gate_grads(gate_acts, cell_state, cell_prev, grad_hidden.reshape(B, HB, BLK), grad_carry)
            partial_value = spread(grad_pre, weight_f, layout_rows)
            return (partial_value[:, H:], carry_new), (grad_pre, partial_value[:, :H])

        start = (jnp.zeros((B, H), jnp.float32), jnp.zeros((B, HB, BLK), jnp.float32))
        rows_in = (d_hidden[layer_idx], from_above, act_seq, cell_seq, prev_seq)
        _, (pre_seq, down_seq) = lax.scan(retreat, start, rows_in, reverse=True)
        picked_all = jnp.take(input_seq, layout_rows, axis=2).astype(jnp.float32)
        grad_w = jnp.einsum("sbjkc,sbjd->jkcd", picked_all, pre_seq.astype(jnp.float32))
        grad_w_all[layer_idx] = grad_w.astype(jnp.bfloat16)
        grad_b_all[layer_idx] = jnp.sum(pre_seq.astype(jnp.float32), axis=(0, 1))
        from_above = down_seq
    return jnp.stack(hidden_all, 0), jnp.stack(grad_w_all, 0), jnp.stack(grad_b_all, 0)
```

```python
import functools

import jax
import jax.numpy as jnp
from jax import lax
from jax.experimental import pallas as pl
from jax.experimental.pallas import tpu as pltpu
from jax.sharding import PartitionSpec as P

MESH = pl.DeviceIdType.MESH
F32 = jnp.float32
BF16 = jnp.bfloat16
INNER = 2


def looped(count, unroll, body):
    while count % unroll:
        unroll -= 1

    def several(step, carry):
        for part in range(unroll):
            body(step * unroll + part)
        return carry

    lax.fori_loop(0, count // unroll, several, 0)


def lstm_kernel(
    layers,
    units,
    groups,
    lay_ref,
    perm_ref,
    same_ref,
    last_ref,
    emb_ref,
    w_hbm,
    bias_ref,
    cot_ref,
    hid_ref,
    g_hbm,
    gp_ref,
    w_ref,
    g_ref,
    x_ref,
    h_ref,
    s_ref,
    act_ref,
    cell_ref,
    c_ref,
    r_ref,
    p_ref,
    xr_ref,
    zr_ref,
    q_ref,
    d_ref,
    ds_ref,
    rec_ref,
    carry_ref,
    w_sem,
    g_sem,
    h_recv,
    s_recv,
    z_send,
    x_send,
    up_send,
    ez_send,
    ex_send,
    xr_recv,
    zr_recv,
    xr_send,
    zr_send,
    d_recv,
    d_send,
):
    layer = lax.axis_index("layer")
    unit = lax.axis_index("unit")
    outer = units // INNER
    zpos = unit // INNER
    xpos = unit % INNER
    partner = zpos * INNER + (1 - xpos)
    steps, rows, _ = cot_ref.shape
    own_blocks, nonzero = lay_ref.shape
    pairs = own_blocks // 2
    half_blocks = units * own_blocks
    entries = own_blocks * nonzero // groups
    per_group = own_blocks // groups
    has_above = layer < layers - 1
    has_below = layer > 0
    low = lax.broadcasted_iota(jnp.int32, (rows, 128), 1) < 64

    def other_z(dz):
        return lax.rem(zpos + dz, outer)

    def swap(tile):
        return pltpu.roll(tile, 64, axis=1)

    def remote(src, dst, send, recv, where_to):
        return pltpu.make_async_remote_copy(
            src_ref=src,
            dst_ref=dst,
            send_sem=send,
            recv_sem=recv,
            device_id=where_to,
            device_id_type=MESH,
        )

    barrier = pltpu.get_barrier_semaphore()

    def greet(where_to):
        pl.semaphore_signal(barrier, inc=1, device_id=where_to, device_id_type=MESH)

    for dz in range(1, outer):
        greet((layer, other_z(dz) * INNER + xpos))
    greet((layer, partner))

    @pl.when(has_above)
    def _():
        greet((layer + 1, unit))

    @pl.when(has_below)
    def _():
        greet((layer - 1, unit))

    pl.semaphore_wait(
        barrier, outer + lax.min(layers - 1 - layer, 1) + lax.min(layer, 1)
    )

    def emb_z(t, dz):
        return remote(
            s_ref.at[t, unit],
            s_ref.at[t, unit],
            ez_send.at[t, dz],
            s_recv.at[t, unit],
            (layer, other_z(dz) * INNER + xpos),
        )

    def emb_x(t, dz):
        v = other_z(dz) * INNER + xpos
        return remote(
            s_ref.at[t, v], s_ref.at[t, v], ex_send.at[t, dz], s_recv.at[t, v], (layer, partner)
        )

    def s_wait(t, v):
        remote(
            s_ref.at[t, v], s_ref.at[t, v], ex_send.at[t, 0], s_recv.at[t, v], (layer, partner)
        ).wait_recv()

    def emb_forward(t):
        for dz in range(1, outer):
            s_wait(t, other_z(dz) * INNER + xpos)
            emb_x(t, dz).start()

    @pl.when(layer == 0)
    def _():
        for t in range(steps):
            s_ref[t, unit] = emb_ref[t]
            for dz in range(1, outer):
                emb_z(t, dz).start()
            emb_x(t, 0).start()

    def w_copy(j):
        return pltpu.make_async_copy(w_hbm.at[j], w_ref.at[j], w_sem.at[j])

    looped(own_blocks, 1, lambda j: w_copy(j).start())

    zero_tile = jnp.zeros((rows, 128), F32)

    def zero_x(b):
        x_ref[half_blocks + b] = jnp.zeros((rows, 128), BF16)

    looped(half_blocks, 8, zero_x)
    for q in range(pairs):
        rec_ref[q] = zero_tile
        carry_ref[q] = zero_tile
        cell_ref[0, q] = zero_tile
    for g in range(groups):
        r_ref[g * (entries + 1) + entries] = zero_tile

    @pl.when(layer == layers - 1)
    def _():
        for t in range(steps):
            for q in range(pairs):
                d_ref[t, q] = jnp.zeros((rows, 128), BF16)

    def unpack(src, t, v, base):
        for q in range(pairs):
            tile = src[t, v, q].astype(F32)
            turned = swap(tile)
            at = base + v * own_blocks + 2 * q
            x_ref[at] = jnp.where(low, tile, turned).astype(BF16)
            x_ref[at + 1] = jnp.where(low, turned, tile).astype(BF16)

    @pl.when(layer == 0)
    def _():
        emb_forward(0)

    looped(own_blocks, 1, lambda j: w_copy(j).wait())

    def own_copy_z(t, dz):
        return remote(
            h_ref.at[t, unit],
            h_ref.at[t, unit],
            z_send.at[dz],
            h_recv.at[t, unit],
            (layer, other_z(dz) * INNER + xpos),
        )

    def copy_x(t, dz):
        v = other_z(dz) * INNER + xpos
        return remote(
            h_ref.at[t, v], h_ref.at[t, v], x_send.at[dz], h_recv.at[t, v], (layer, partner)
        )

    def copy_up(t, v):
        return remote(
            h_ref.at[t, v], s_ref.at[t, v], up_send.at[v], s_recv.at[t, v], (layer + 1, unit)
        )

    def h_wait(t, v):
        remote(
            h_ref.at[t, v], h_ref.at[t, v], x_send.at[0], h_recv.at[t, v], (layer, partner)
        ).wait_recv()

    def wait_up(t):
        @pl.when((layers - 1 - layer) * (t + 1) > 0)
        def _():
            looped(units, 1, lambda v: copy_up(t, v).wait_send())

    def forward(t, carry):
        def take_source(i):
            v = lax.rem(unit + i, units)

            @pl.when(layer + lax.abs(lax.rem(v, INNER) - xpos) > 0)
            def _():
                s_wait(t, v)

            unpack(s_ref, t, v, 0)

        looped(units, 1, take_source)

        def cells(q):
            pres = []
            for side in range(2):
                j = 2 * q + side
                tiles = []
                for k in range(0, nonzero, 2):
                    tiles.append(
                        jnp.where(low, x_ref[lay_ref[j, k]], x_ref[lay_ref[j, k + 1]])
                    )
                picked = jnp.concatenate(tiles, axis=1)
                g_ref[j, pl.ds(pl.multiple_of(t * rows, rows), rows), :] = picked
                pres.append(
                    jnp.dot(picked, w_ref[j], preferred_element_type=F32)
                    + bias_ref[pl.ds(j, 1), :]
                )
            first, second = pres
            i_pre = jnp.where(low, first[:, :128], swap(second[:, :128]))
            f_pre = jnp.where(low, swap(first[:, :128]), second[:, :128])
            u_pre = jnp.where(low, first[:, 128:], swap(second[:, 128:]))
            o_pre = jnp.where(low, swap(first[:, 128:]), second[:, 128:])
            in_gate = jax.nn.sigmoid(i_pre)
            forget = jax.nn.sigmoid(f_pre)
            update = jnp.tanh(u_pre)
            out_gate = jax.nn.sigmoid(o_pre)
            cell = forget * cell_ref[t, q] + in_gate * update
            squash = jnp.tanh(cell)
            hidden = (out_gate * squash).astype(BF16)
            cell_ref[t + 1, q] = cell
            act_ref[0, t, q] = in_gate
            act_ref[1, t, q] = forget
            act_ref[2, t, q] = update
            act_ref[3, t, q] = out_gate
            act_ref[4, t, q] = squash
            h_ref[t, unit, q] = hidden
            hid_ref[t, :, pl.ds(pl.multiple_of(q * 128, 128), 128)] = hidden

        looped(pairs, 2, cells)

        wait_up(t - 1)

        @pl.when((layers - 1 - layer) + (steps - 1 - t) > 0)
        def _():
            for dz in range(1, outer):
                own_copy_z(t, dz).start()
            copy_x(t, 0).start()

            @pl.when(has_above)
            def _():
                copy_up(t, unit).start()

            @pl.when(layer + lax.div(t + 1, steps) == 0)
            def _():
                emb_forward(t + 1)

            unpack(h_ref, t, unit, half_blocks)

            def arrived(dz, is_partner):
                v = other_z(dz) * INNER + (1 - xpos if is_partner else xpos)
                h_wait(t, v)
                if not is_partner:
                    copy_x(t, dz).start()

                @pl.when(has_above)
                def _():
                    copy_up(t, v).start()

                unpack(h_ref, t, v, half_blocks)

            looped(outer - 1, 1, lambda i: arrived(i + 1, False))
            looped(outer, 1, lambda i: arrived(i, True))
            for dz in range(1, outer):
                own_copy_z(t, dz).wait_send()
            for dz in range(outer):
                copy_x(t, dz).wait_send()

        return carry

    lax.fori_loop(0, steps, forward, 0)
    g_copy = pltpu.make_async_copy(g_ref, g_hbm, g_sem)
    g_copy.start()
    wait_up(steps - 1)

    @pl.when(layer == 0)
    def _():
        for t in range(steps):
            for dz in range(1, outer):
                emb_z(t, dz).wait_send()
            for dz in range(outer):
                emb_x(t, dz).wait_send()

    def group_sum(half, v, q):
        at = half * half_blocks + v * own_blocks + 2 * q
        left = right = None
        for g in range(groups):
            one = r_ref[last_ref[g, at]]
            two = r_ref[last_ref[g, at + 1]]
            left = one if left is None else left + one
            right = two if right is None else right + two
        return jnp.where(low, left, right)

    def copy_xr(t, half, z):
        return remote(
            p_ref.at[half, z],
            xr_ref.at[t, half, z],
            xr_send.at[half, z],
            xr_recv.at[t, half, z],
            (layer, partner),
        )

    def copy_zr(t, half, dz):
        z = other_z(dz)
        return remote(
            q_ref.at[half, z],
            zr_ref.at[t, half, zpos],
            zr_send.at[half, z],
            zr_recv.at[t, half, zpos],
            (layer, z * INNER + xpos),
        )

    def wait_zr(t, half, dz):
        z = other_z(dz)
        remote(
            q_ref.at[half, z],
            zr_ref.at[t, half, z],
            zr_send.at[half, z],
            zr_recv.at[t, half, z],
            (layer, z * INNER + xpos),
        ).wait_recv()

    def copy_down(t):
        return remote(ds_ref, d_ref.at[t], d_send, d_recv.at[t], (layer - 1, unit))

    def backward(i, carry):
        t = steps - 1 - i

        @pl.when(has_above)
        def _():
            remote(ds_ref, d_ref.at[t], d_send, d_recv.at[t], (layer + 1, unit)).wait_recv()

        def cells(q):
            grad_hidden = (
                cot_ref[t, :, pl.ds(pl.multiple_of(q * 128, 128), 128)].astype(F32)
                + d_ref[t, q].astype(F32)
                + rec_ref[q]
            )
            in_gate = act_ref[0, t, q]
            forget = act_ref[1, t, q]
            update = act_ref[2, t, q]
            out_gate = act_ref[3, t, q]
            squash = act_ref[4, t, q]
            grad_cell = carry_ref[q] + grad_hidden * out_gate * (1.0 - squash * squash)
            gi = grad_cell * update * in_gate * (1.0 - in_gate)
            gf = grad_cell * cell_ref[t, q] * forget * (1.0 - forget)
            gu = grad_cell * in_gate * (1.0 - update * update)
            go = grad_hidden * squash * out_gate * (1.0 - out_gate)
            carry_ref[q] = grad_cell * forget
            at = pl.ds(pl.multiple_of(t * rows, rows), rows)
            gp_ref[2 * q, at, :128] = jnp.where(low, gi, swap(gf)).astype(BF16)
            gp_ref[2 * q, at, 128:] = jnp.where(low, gu, swap(go)).astype(BF16)
            gp_ref[2 * q + 1, at, :128] = jnp.where(low, swap(gi), gf).astype(BF16)
            gp_ref[2 * q + 1, at, 128:] = jnp.where(low, swap(gu), go).astype(BF16)

        looped(pairs, 2, cells)

        @pl.when(layer + t > 0)
        def _():
            def two_groups(gg, inner_carry):
                def contributions(jl):
                    j = gg * (2 * per_group) + jl
                    grad_pre = gp_ref[j, pl.ds(pl.multiple_of(t * rows, rows), rows), :]
                    contrib = lax.dot_general(
                        grad_pre, w_ref[j], (((1,), (1,)), ((), ())), preferred_element_type=F32
                    )
                    for k in range(0, nonzero, 2):
                        tile = contrib[:, k * 64 : k * 64 + 128]
                        turned = swap(tile)
                        c_ref[jl * nonzero + k] = jnp.where(low, tile, turned)
                        c_ref[jl * nonzero + k + 1] = jnp.where(low, turned, tile)

                looped(2 * per_group, 2, contributions)

                def runs(r8, run):
                    run = list(run)
                    for part in range(8):
                        r = r8 * 8 + part
                        for side in range(2):
                            g = gg * 2 + side
                            run[side] = c_ref[perm_ref[g, r]] + same_ref[g, r] * run[side]
                            r_ref[g * (entries + 1) + r] = run[side]
                    return tuple(run)

                lax.fori_loop(0, entries // 8, runs, (zero_tile, zero_tile))
                return inner_carry

            lax.fori_loop(0, groups // 2, two_groups, 0)

            def per_half(do):
                @pl.when(t > 0)
                def _():
                    do(1)

                @pl.when(has_below)
                def _():
                    do(0)

            def send_partner(half):
                def one(i):
                    z = other_z(lax.rem(i + 1, outer))
                    for q in range(pairs):
                        p_ref[half, z, q] = group_sum(
                            half, z * INNER + (1 - xpos), q
                        ).astype(BF16)
                    copy_xr(t, half, z).start()

                looped(outer, 1, one)

            def send_along(half):
                def one(i):
                    dz = i + 1
                    z = other_z(dz)
                    copy_xr(t, half, z).wait_recv()
                    for q in range(pairs):
                        q_ref[half, z, q] = (
                            group_sum(half, z * INNER + xpos, q)
                            + xr_ref[t, half, z, q].astype(F32)
                        ).astype(BF16)
                    copy_zr(t, half, dz).start()

                looped(outer - 1, 1, one)

            def finish(half):
                copy_xr(t, half, zpos).wait_recv()
                for dz in range(1, outer):
                    wait_zr(t, half, dz)

                def one(q):
                    total = group_sum(half, unit, q) + xr_ref[t, half, zpos, q].astype(F32)
                    for dz in range(1, outer):
                        total = total + zr_ref[t, half, other_z(dz), q].astype(F32)
                    if half:
                        rec_ref[q] = total
                    else:
                        ds_ref[q] = total.astype(BF16)

                looped(pairs, 2, one)
                if not half:
                    copy_down(t).start()

            def settle(half):
                for z in range(outer):
                    copy_xr(t, half, z).wait_send()
                for dz in range(1, outer):
                    copy_zr(t, half, dz).wait_send()
                if not half:
                    copy_down(t).wait_send()

            per_half(send_partner)
            per_half(send_along)
            per_half(finish)
            per_half(settle)

        return carry

    lax.fori_loop(0, steps, backward, 0)
    g_copy.wait()


def weight_kernel(g_ref, gp_ref, gw_ref, gb_ref):
    grad_pre = gp_ref[0]
    gw_ref[0] = lax.dot_general(
        g_ref[0], grad_pre, (((0,), (0,)), ((), ())), preferred_element_type=F32
    ).astype(BF16)
    gb_ref[0] = jnp.sum(grad_pre.astype(F32), axis=0, keepdims=True)


def on_device(layers, units, tokens, embed, weights, layout, bias, d_hidden):
    steps, rows = tokens.shape
    vocab, width = embed.shape
    _, own_blocks, nonzero, block, gates = weights.shape
    pairs = own_blocks // 2
    half_blocks = units * own_blocks
    groups = 4 if own_blocks % 4 == 0 else 2
    entries = own_blocks * nonzero // groups
    outer = units // INNER
    depth = nonzero * block

    onehot = (tokens.reshape(-1)[:, None] == jnp.arange(vocab, dtype=jnp.int32)).astype(BF16)
    looked = jnp.dot(onehot, embed, preferred_element_type=F32).astype(BF16)
    emb = looked.reshape(steps, rows, pairs, 128).transpose(0, 2, 1, 3)

    lay = layout[0]
    ent = lay.reshape(groups, entries)
    spot = jnp.arange(entries, dtype=jnp.int32)
    key = ent * entries + spot
    rank = jnp.sum((key[:, None, :] < key[:, :, None]).astype(jnp.int32), -1)
    placed = rank[:, :, None] == spot
    perm = jnp.sum(jnp.where(placed, spot[:, None], 0), 1)
    ordered = jnp.sum(jnp.where(placed, ent[:, :, None], 0), 1)
    same = jnp.concatenate(
        [jnp.zeros((groups, 1), F32), (ordered[:, 1:] == ordered[:, :-1]).astype(F32)], 1
    )
    group_ids = jnp.arange(groups, dtype=jnp.int32)[:, None]
    perm = perm + (group_ids % 2) * entries
    blocks = jnp.arange(2 * half_blocks, dtype=jnp.int32)[:, None]
    below = jnp.sum((ent[:, None, :] <= blocks).astype(jnp.int32), -1)
    present = jnp.any(ent[:, None, :] == blocks, -1)
    last = jnp.where(present, below - 1, entries) + group_ids * (entries + 1)

    smem = pl.BlockSpec(memory_space=pltpu.SMEM)
    vmem = pl.BlockSpec(memory_space=pltpu.VMEM)
    hbm = pl.BlockSpec(memory_space=pl.ANY)
    tile = (rows, 128)
    dma = pltpu.SemaphoreType.DMA
    hidden, picked, grad_pre = pl.pallas_call(
        functools.partial(lstm_kernel, layers, units, groups),
        out_shape=(
            jax.ShapeDtypeStruct((steps, rows, width), BF16),
            jax.ShapeDtypeStruct((own_blocks, steps * rows, depth), BF16),
            jax.ShapeDtypeStruct((own_blocks, steps * rows, gates), BF16),
        ),
        in_specs=[smem, smem, smem, smem, vmem, hbm, vmem, vmem],
        out_specs=(vmem, hbm, vmem),
        scratch_shapes=[
            pltpu.VMEM((own_blocks, depth, gates), BF16),
            pltpu.VMEM((own_blocks, steps * rows, depth), BF16),
            pltpu.VMEM((2 * half_blocks,) + tile, BF16),
            pltpu.VMEM((steps, units, pairs) + tile, BF16),
            pltpu.VMEM((steps, units, pairs) + tile, BF16),
            pltpu.VMEM((5, steps, pairs) + tile, F32),
            pltpu.VMEM((steps + 1, pairs) + tile, F32),
            pltpu.VMEM((2 * entries,) + tile, F32),
            pltpu.VMEM((groups * (entries + 1),) + tile, F32),
            pltpu.VMEM((2, outer, pairs) + tile, BF16),
            pltpu.VMEM((steps, 2, outer, pairs) + tile, BF16),
            pltpu.VMEM((steps, 2, outer, pairs) + tile, BF16),
            pltpu.VMEM((2, outer, pairs) + tile, BF16),
            pltpu.VMEM((steps, pairs) + tile, BF16),
            pltpu.VMEM((pairs,) + tile, BF16),
            pltpu.VMEM((pairs,) + tile, F32),
            pltpu.VMEM((pairs,) + tile, F32),
            dma((own_blocks,)),
            dma,
            dma((steps, units)),
            dma((steps, units)),
            dma((outer,)),
            dma((outer,)),
            dma((units,)),
            dma((steps, outer)),
            dma((steps, outer)),
            dma((steps, 2, outer)),
            dma((steps, 2, outer)),
            dma((2, outer)),
            dma((2, outer)),
            dma((steps,)),
            dma,
        ],
        compiler_params=pltpu.CompilerParams(
            collective_id=0, has_side_effects=True, vmem_limit_bytes=60 * 2**20
        ),
        name="lstm",
    )(lay, perm, same, last, emb, weights[0].reshape(own_blocks, depth, gates), bias[0], d_hidden[0])

    grad_w, grad_b = pl.pallas_call(
        weight_kernel,
        grid=(own_blocks,),
        out_shape=(
            jax.ShapeDtypeStruct((own_blocks, depth, gates), BF16),
            jax.ShapeDtypeStruct((own_blocks, 1, gates), F32),
        ),
        in_specs=[
            pl.BlockSpec((1, steps * rows, depth), lambda j: (j, 0, 0)),
            pl.BlockSpec((1, steps * rows, gates), lambda j: (j, 0, 0)),
        ],
        out_specs=(
            pl.BlockSpec((1, depth, gates), lambda j: (j, 0, 0)),
            pl.BlockSpec((1, 1, gates), lambda j: (j, 0, 0)),
        ),
        name="grad_weights",
    )(picked, grad_pre)
    return (
        hidden[None],
        grad_w.reshape(1, own_blocks, nonzero, block, gates),
        grad_b.reshape(1, own_blocks, gates),
    )


def solution(mesh):
    placed = (
        P(),
        P(None, "unit"),
        P("layer", "unit", None, None, None),
        P("layer", "unit", None),
        P("layer", "unit", None),
        P("layer", None, None, "unit"),
    )
    return jax.shard_map(
        functools.partial(on_device, mesh.shape["layer"], mesh.shape["unit"]),
        mesh=mesh,
        in_specs=placed,
        out_specs=(
            P("layer", None, None, "unit"),
            P("layer", "unit", None, None, None),
            P("layer", "unit", None),
        ),
        check_vma=False,
    )
```

```python
import functools

import jax
import jax.numpy as jnp
from jax import lax
from jax.experimental import pallas as pl
from jax.experimental.pallas import tpu as pltpu
from jax.sharding import PartitionSpec as P

MESH = pl.DeviceIdType.MESH
F32 = jnp.float32
BF16 = jnp.bfloat16
INNER = 2
SUBS = 2


def looped(count, unroll, body):
    while count % unroll:
        unroll -= 1

    def several(step, carry):
        for part in range(unroll):
            body(step * unroll + part)
        return carry

    lax.fori_loop(0, count // unroll, several, 0)


def lstm_kernel(
    layers,
    units,
    groups,
    lay_ref,
    perm_ref,
    same_ref,
    last_ref,
    emb_ref,
    w_hbm,
    bias_ref,
    cot_ref,
    hid_ref,
    xt_hbm,
    gp_ref,
    w_ref,
    xt_ref,
    x_ref,
    h_ref,
    s_ref,
    act_ref,
    cell_ref,
    c_ref,
    r_ref,
    p_ref,
    xr_ref,
    zr_ref,
    q_ref,
    d_ref,
    ds_ref,
    rec_ref,
    carry_ref,
    w_sem,
    xt_sem,
    h_recv,
    s_recv,
    z_send,
    x_send,
    up_send,
    ez_send,
    ex_send,
    xr_recv,
    zr_recv,
    xr_send,
    zr_send,
    d_recv,
    d_send,
):
    layer = lax.axis_index("layer")
    unit = lax.axis_index("unit")
    outer = units // INNER
    zpos = unit // INNER
    xpos = unit % INNER
    partner = zpos * INNER + (1 - xpos)
    steps, rows, _ = cot_ref.shape
    own_blocks, nonzero = lay_ref.shape
    pairs = own_blocks // 2
    sub_pairs = pairs // SUBS
    half_blocks = units * own_blocks
    entries = own_blocks * nonzero // groups
    per_group = own_blocks // groups
    has_above = layer < layers - 1
    has_below = layer > 0
    low = lax.broadcasted_iota(jnp.int32, (rows, 128), 1) < 64

    def other_z(dz):
        return lax.rem(zpos + dz, outer)

    def swap(tile):
        return pltpu.roll(tile, 64, axis=1)

    def remote(src, dst, send, recv, where_to):
        return pltpu.make_async_remote_copy(
            src_ref=src,
            dst_ref=dst,
            send_sem=send,
            recv_sem=recv,
            device_id=where_to,
            device_id_type=MESH,
        )

    barrier = pltpu.get_barrier_semaphore()

    def greet(where_to):
        pl.semaphore_signal(barrier, inc=1, device_id=where_to, device_id_type=MESH)

    for dz in range(1, outer):
        greet((layer, other_z(dz) * INNER + xpos))
    greet((layer, partner))

    @pl.when(has_above)
    def _():
        greet((layer + 1, unit))

    @pl.when(has_below)
    def _():
        greet((layer - 1, unit))

    pl.semaphore_wait(
        barrier, outer + lax.min(layers - 1 - layer, 1) + lax.min(layer, 1)
    )

    def part(ref, t, v, sub):
        return ref.at[t, v, pl.ds(sub * sub_pairs, sub_pairs)]

    def emb_z(t, dz, sub):
        here = part(s_ref, t, unit, sub)
        return remote(
            here,
            here,
            ez_send.at[t, dz, sub],
            s_recv.at[t, unit, sub],
            (layer, other_z(dz) * INNER + xpos),
        )

    def emb_x(t, dz, sub):
        v = other_z(dz) * INNER + xpos
        here = part(s_ref, t, v, sub)
        return remote(here, here, ex_send.at[t, dz, sub], s_recv.at[t, v, sub], (layer, partner))

    def s_wait(t, v, sub):
        here = part(s_ref, t, v, sub)
        remote(
            here, here, ex_send.at[t, 0, sub], s_recv.at[t, v, sub], (layer, partner)
        ).wait_recv()

    def emb_forward(t):
        for sub in range(SUBS):
            for dz in range(1, outer):
                s_wait(t, other_z(dz) * INNER + xpos, sub)
                emb_x(t, dz, sub).start()

    @pl.when(layer == 0)
    def _():
        for t in range(steps):
            s_ref[t, unit] = emb_ref[t]
            for sub in range(SUBS):
                for dz in range(1, outer):
                    emb_z(t, dz, sub).start()
                emb_x(t, 0, sub).start()

    def w_copy(j):
        return pltpu.make_async_copy(w_hbm.at[j], w_ref.at[j], w_sem.at[j])

    looped(own_blocks, 1, lambda j: w_copy(j).start())

    zero_tile = jnp.zeros((rows, 128), F32)

    def zero_x(b):
        x_ref[half_blocks + b] = jnp.zeros((rows, 128), BF16)

    looped(half_blocks, 8, zero_x)
    for q in range(pairs):
        rec_ref[q] = zero_tile
        carry_ref[q] = zero_tile
        cell_ref[0, q] = zero_tile
    for g in range(groups):
        r_ref[g * (entries + 1) + entries] = zero_tile.astype(BF16)

    @pl.when(layer == layers - 1)
    def _():
        for t in range(steps):
            for q in range(pairs):
                d_ref[t, q] = jnp.zeros((rows, 128), BF16)

    def unpack(src, t, v, base, sub):
        for part_q in range(sub_pairs):
            q = sub * sub_pairs + part_q
            tile = src[t, v, q].astype(F32)
            turned = swap(tile)
            at = base + v * own_blocks + 2 * q
            x_ref[at] = jnp.where(low, tile, turned).astype(BF16)
            x_ref[at + 1] = jnp.where(low, turned, tile).astype(BF16)

    @pl.when(layer == 0)
    def _():
        emb_forward(0)

    looped(own_blocks, 1, lambda j: w_copy(j).wait())

    def own_copy_z(t, dz, sub):
        here = part(h_ref, t, unit, sub)
        return remote(
            here,
            here,
            z_send.at[dz, sub],
            h_recv.at[t, unit, sub],
            (layer, other_z(dz) * INNER + xpos),
        )

    def copy_x(t, dz, sub):
        v = other_z(dz) * INNER + xpos
        here = part(h_ref, t, v, sub)
        return remote(here, here, x_send.at[dz, sub], h_recv.at[t, v, sub], (layer, partner))

    def copy_up(t, v, sub):
        return remote(
            part(h_ref, t, v, sub),
            part(s_ref, t, v, sub),
            up_send.at[v, sub],
            s_recv.at[t, v, sub],
            (layer + 1, unit),
        )

    def h_wait(t, v, sub):
        here = part(h_ref, t, v, sub)
        remote(
            here, here, x_send.at[0, sub], h_recv.at[t, v, sub], (layer, partner)
        ).wait_recv()

    def wait_up(t):
        @pl.when((layers - 1 - layer) * (t + 1) > 0)
        def _():
            def one(v):
                for sub in range(SUBS):
                    copy_up(t, v, sub).wait_send()

            looped(units, 1, one)

    def forward(t, carry):
        def take_source(i):
            v = lax.rem(unit + i, units)

            @pl.when(layer + lax.abs(lax.rem(v, INNER) - xpos) > 0)
            def _():
                for sub in range(SUBS):
                    s_wait(t, v, sub)

            for sub in range(SUBS):
                unpack(s_ref, t, v, 0, sub)

        looped(units, 1, take_source)

        def cells(q):
            pres = []
            for side in range(2):
                j = 2 * q + side
                tiles = []
                for k in range(0, nonzero, 2):
                    tiles.append(
                        jnp.where(low, x_ref[lay_ref[j, k]], x_ref[lay_ref[j, k + 1]])
                    )
                picked = jnp.concatenate(tiles, axis=1)
                pres.append(
                    jnp.dot(picked, w_ref[j], preferred_element_type=F32)
                    + bias_ref[pl.ds(j, 1), :]
                )
            first, second = pres
            i_pre = jnp.where(low, first[:, :128], swap(second[:, :128]))
            f_pre = jnp.where(low, swap(first[:, :128]), second[:, :128])
            u_pre = jnp.where(low, first[:, 128:], swap(second[:, 128:]))
            o_pre = jnp.where(low, swap(first[:, 128:]), second[:, 128:])
            in_gate = jax.nn.sigmoid(i_pre)
            forget = jax.nn.sigmoid(f_pre)
            update = jnp.tanh(u_pre)
            out_gate = jax.nn.sigmoid(o_pre)
            cell = forget * cell_ref[t, q] + in_gate * update
            squash = jnp.tanh(cell)
            hidden = (out_gate * squash).astype(BF16)
            cell_ref[t + 1, q] = cell
            act_ref[0, t, q] = in_gate
            act_ref[1, t, q] = forget
            act_ref[2, t, q] = update
            act_ref[3, t, q] = out_gate
            act_ref[4, t, q] = squash
            h_ref[t, unit, q] = hidden
            hid_ref[t, :, pl.ds(pl.multiple_of(q * 128, 128), 128)] = hidden

        wait_up(t - 1)
        for sub in range(SUBS):
            looped(sub_pairs, 2, lambda i: cells(sub * sub_pairs + i))

            @pl.when((layers - 1 - layer) + (steps - 1 - t) > 0)
            def _():
                for dz in range(1, outer):
                    own_copy_z(t, dz, sub).start()
                copy_x(t, 0, sub).start()

                @pl.when(has_above)
                def _():
                    copy_up(t, unit, sub).start()

        @pl.when((layers - 1 - layer) + (steps - 1 - t) > 0)
        def _():
            for sub in range(SUBS):
                unpack(h_ref, t, unit, half_blocks, sub)

            def arrived(dz, sub, is_partner):
                v = other_z(dz) * INNER + (1 - xpos if is_partner else xpos)
                h_wait(t, v, sub)
                if not is_partner:
                    copy_x(t, dz, sub).start()

                @pl.when(has_above)
                def _():
                    copy_up(t, v, sub).start()

                unpack(h_ref, t, v, half_blocks, sub)

            for sub in range(SUBS):
                looped(outer - 1, 1, lambda i: arrived(i + 1, sub, False))

            @pl.when(layer + lax.div(t + 1, steps) == 0)
            def _():
                emb_forward(t + 1)

            for sub in range(SUBS):
                looped(outer, 1, lambda i: arrived(i, sub, True))
            for sub in range(SUBS):
                for dz in range(1, outer):
                    own_copy_z(t, dz, sub).wait_send()
                for dz in range(outer):
                    copy_x(t, dz, sub).wait_send()

        return carry

    lax.fori_loop(0, steps, forward, 0)
    wait_up(steps - 1)

    xt_copy = pltpu.make_async_copy(xt_ref, xt_hbm, xt_sem)

    def turn_inputs():
        def one(at):
            v = at // pairs
            q = at % pairs
            source = jnp.concatenate([s_ref[t, v, q] for t in range(steps)], axis=0).T
            recur = jnp.concatenate(
                [jnp.zeros((rows, 128), BF16)] + [h_ref[t, v, q] for t in range(steps - 1)],
                axis=0,
            ).T
            for side in range(2):
                xt_ref[2 * at + side] = source[side * 64 : side * 64 + 64]
                xt_ref[half_blocks + 2 * at + side] = recur[side * 64 : side * 64 + 64]

        looped(units * pairs, 2, one)
        xt_copy.start()

    @pl.when(has_above)
    def _():
        turn_inputs()

    @pl.when(layer == 0)
    def _():
        for t in range(steps):
            for sub in range(SUBS):
                for dz in range(1, outer):
                    emb_z(t, dz, sub).wait_send()
                for dz in range(outer):
                    emb_x(t, dz, sub).wait_send()

    def group_sum(half, v, q):
        at = half * half_blocks + v * own_blocks + 2 * q
        total = None
        for g in range(groups):
            both = jnp.where(low, r_ref[last_ref[g, at]], r_ref[last_ref[g, at + 1]])
            both = both.astype(F32)
            total = both if total is None else total + both
        return total

    def copy_xr(t, half, z):
        return remote(
            p_ref.at[half, z],
            xr_ref.at[t, half, z],
            xr_send.at[half, z],
            xr_recv.at[t, half, z],
            (layer, partner),
        )

    def copy_zr(t, half, dz):
        z = other_z(dz)
        return remote(
            q_ref.at[half, z],
            zr_ref.at[t, half, zpos],
            zr_send.at[half, z],
            zr_recv.at[t, half, zpos],
            (layer, z * INNER + xpos),
        )

    def wait_zr(t, half, dz):
        z = other_z(dz)
        remote(
            q_ref.at[half, z],
            zr_ref.at[t, half, z],
            zr_send.at[half, z],
            zr_recv.at[t, half, z],
            (layer, z * INNER + xpos),
        ).wait_recv()

    def copy_down(t):
        return remote(ds_ref, d_ref.at[t], d_send, d_recv.at[t], (layer - 1, unit))

    def backward(i, carry):
        t = steps - 1 - i

        @pl.when(has_above)
        def _():
            remote(ds_ref, d_ref.at[t], d_send, d_recv.at[t], (layer + 1, unit)).wait_recv()

        def cells(q):
            grad_hidden = (
                cot_ref[t, :, pl.ds(pl.multiple_of(q * 128, 128), 128)].astype(F32)
                + d_ref[t, q].astype(F32)
                + rec_ref[q]
            )
            in_gate = act_ref[0, t, q]
            forget = act_ref[1, t, q]
            update = act_ref[2, t, q]
            out_gate = act_ref[3, t, q]
            squash = act_ref[4, t, q]
            grad_cell = carry_ref[q] + grad_hidden * out_gate * (1.0 - squash * squash)
            gi = grad_cell * update * in_gate * (1.0 - in_gate)
            gf = grad_cell * cell_ref[t, q] * forget * (1.0 - forget)
            gu = grad_cell * in_gate * (1.0 - update * update)
            go = grad_hidden * squash * out_gate * (1.0 - out_gate)
            carry_ref[q] = grad_cell * forget
            at = pl.ds(pl.multiple_of(t * rows, rows), rows)
            gp_ref[2 * q, at, :128] = jnp.where(low, gi, swap(gf)).astype(BF16)
            gp_ref[2 * q, at, 128:] = jnp.where(low, gu, swap(go)).astype(BF16)
            gp_ref[2 * q + 1, at, :128] = jnp.where(low, swap(gi), gf).astype(BF16)
            gp_ref[2 * q + 1, at, 128:] = jnp.where(low, swap(gu), go).astype(BF16)

        looped(pairs, 2, cells)

        @pl.when(layer + t > 0)
        def _():
            def two_groups(gg, inner_carry):
                def contributions(jl):
                    j = gg * (2 * per_group) + jl
                    grad_pre = gp_ref[j, pl.ds(pl.multiple_of(t * rows, rows), rows), :]
                    contrib = lax.dot_general(
                        grad_pre, w_ref[j], (((1,), (1,)), ((), ())), preferred_element_type=F32
                    )
                    for k in range(0, nonzero, 2):
                        tile = contrib[:, k * 64 : k * 64 + 128]
                        turned = swap(tile)
                        c_ref[jl * nonzero + k] = jnp.where(low, tile, turned).astype(BF16)
                        c_ref[jl * nonzero + k + 1] = jnp.where(low, turned, tile).astype(BF16)

                looped(2 * per_group, 2, contributions)

                def runs(r8, run):
                    run = list(run)
                    for part in range(8):
                        r = r8 * 8 + part
                        for side in range(2):
                            g = gg * 2 + side
                            keep = jnp.full((rows, 128), same_ref[g, r], F32).astype(BF16)
                            run[side] = c_ref[perm_ref[g, r]] + keep * run[side]
                            r_ref[g * (entries + 1) + r] = run[side]
                    return tuple(run)

                zero_run = zero_tile.astype(BF16)
                lax.fori_loop(0, entries // 8, runs, (zero_run, zero_run))
                return inner_carry

            lax.fori_loop(0, groups // 2, two_groups, 0)

            def per_half(do):
                @pl.when(t > 0)
                def _():
                    do(1)

                @pl.when(has_below)
                def _():
                    do(0)

            def send_partner(half):
                def one(i):
                    z = other_z(lax.rem(i + 1, outer))
                    for q in range(pairs):
                        p_ref[half, z, q] = group_sum(
                            half, z * INNER + (1 - xpos), q
                        ).astype(BF16)
                    copy_xr(t, half, z).start()

                looped(outer, 1, one)

            def send_along(half):
                def one(i):
                    dz = i + 1
                    z = other_z(dz)
                    copy_xr(t, half, z).wait_recv()
                    for q in range(pairs):
                        q_ref[half, z, q] = (
                            group_sum(half, z * INNER + xpos, q)
                            + xr_ref[t, half, z, q].astype(F32)
                        ).astype(BF16)
                    copy_zr(t, half, dz).start()

                looped(outer - 1, 1, one)

            def finish(half):
                copy_xr(t, half, zpos).wait_recv()
                for dz in range(1, outer):
                    wait_zr(t, half, dz)

                def one(q):
                    total = group_sum(half, unit, q) + xr_ref[t, half, zpos, q].astype(F32)
                    for dz in range(1, outer):
                        total = total + zr_ref[t, half, other_z(dz), q].astype(F32)
                    if half:
                        rec_ref[q] = total
                    else:
                        ds_ref[q] = total.astype(BF16)

                looped(pairs, 2, one)
                if not half:
                    copy_down(t).start()

            def settle(half):
                for z in range(outer):
                    copy_xr(t, half, z).wait_send()
                for dz in range(1, outer):
                    copy_zr(t, half, dz).wait_send()
                if not half:
                    copy_down(t).wait_send()

            per_half(send_partner)
            per_half(send_along)
            per_half(finish)
            per_half(settle)

        return carry

    lax.fori_loop(0, steps, backward, 0)

    @pl.when(layer == layers - 1)
    def _():
        turn_inputs()

    xt_copy.wait()


def weight_kernel(lay_ref, xt_ref, gp_ref, hid_ref, gw_ref, gb_ref, out_ref):
    j = pl.program_id(0)
    grad_pre = gp_ref[0]
    picked = jnp.concatenate(
        [xt_ref[lay_ref[j, k]] for k in range(lay_ref.shape[1])], axis=0
    )
    gw_ref[0] = jnp.dot(picked, grad_pre, preferred_element_type=F32).astype(BF16)
    gb_ref[pl.ds(j, 1), :] = jnp.sum(grad_pre.astype(F32), axis=0, keepdims=True)

    @pl.when(j == 0)
    def _():
        out_ref[...] = hid_ref[...]


def on_device(layers, units, tokens, embed, weights, layout, bias, d_hidden):
    steps, rows = tokens.shape
    vocab, width = embed.shape
    _, own_blocks, nonzero, block, gates = weights.shape
    pairs = own_blocks // 2
    half_blocks = units * own_blocks
    groups = 4 if own_blocks % 4 == 0 else 2
    entries = own_blocks * nonzero // groups
    outer = units // INNER
    depth = nonzero * block

    onehot = (tokens.reshape(-1)[:, None] == jnp.arange(vocab, dtype=jnp.int32)).astype(BF16)
    looked = jnp.dot(onehot, embed, preferred_element_type=F32).astype(BF16)
    emb = looked.reshape(steps, rows, pairs, 128).transpose(0, 2, 1, 3)

    lay = layout[0]
    ent = lay.reshape(groups, entries)
    spot = jnp.arange(entries, dtype=jnp.int32)
    key = ent * entries + spot
    rank = jnp.sum((key[:, None, :] < key[:, :, None]).astype(jnp.int32), -1)
    placed = rank[:, :, None] == spot
    perm = jnp.sum(jnp.where(placed, spot[:, None], 0), 1)
    ordered = jnp.sum(jnp.where(placed, ent[:, :, None], 0), 1)
    same = jnp.concatenate(
        [jnp.zeros((groups, 1), F32), (ordered[:, 1:] == ordered[:, :-1]).astype(F32)], 1
    )
    group_ids = jnp.arange(groups, dtype=jnp.int32)[:, None]
    perm = perm + (group_ids % 2) * entries
    blocks = jnp.arange(2 * half_blocks, dtype=jnp.int32)[:, None]
    below = jnp.sum((ent[:, None, :] <= blocks).astype(jnp.int32), -1)
    present = jnp.any(ent[:, None, :] == blocks, -1)
    last = jnp.where(present, below - 1, entries) + group_ids * (entries + 1)

    smem = pl.BlockSpec(memory_space=pltpu.SMEM)
    vmem = pl.BlockSpec(memory_space=pltpu.VMEM)
    hbm = pl.BlockSpec(memory_space=pl.ANY)
    tile = (rows, 128)
    dma = pltpu.SemaphoreType.DMA
    hidden, inputs_t, grad_pre = pl.pallas_call(
        functools.partial(lstm_kernel, layers, units, groups),
        out_shape=(
            jax.ShapeDtypeStruct((steps, rows, width), BF16),
            jax.ShapeDtypeStruct((2 * half_blocks, block, steps * rows), BF16),
            jax.ShapeDtypeStruct((own_blocks, steps * rows, gates), BF16),
        ),
        in_specs=[smem, smem, smem, smem, vmem, hbm, vmem, vmem],
        out_specs=(vmem, hbm, vmem),
        scratch_shapes=[
            pltpu.VMEM((own_blocks, depth, gates), BF16),
            pltpu.VMEM((2 * half_blocks, block, steps * rows), BF16),
            pltpu.VMEM((2 * half_blocks,) + tile, BF16),
            pltpu.VMEM((steps, units, pairs) + tile, BF16),
            pltpu.VMEM((steps, units, pairs) + tile, BF16),
            pltpu.VMEM((5, steps, pairs) + tile, F32),
            pltpu.VMEM((steps + 1, pairs) + tile, F32),
            pltpu.VMEM((2 * entries,) + tile, BF16),
            pltpu.VMEM((groups * (entries + 1),) + tile, BF16),
            pltpu.VMEM((2, outer, pairs) + tile, BF16),
            pltpu.VMEM((steps, 2, outer, pairs) + tile, BF16),
            pltpu.VMEM((steps, 2, outer, pairs) + tile, BF16),
            pltpu.VMEM((2, outer, pairs) + tile, BF16),
            pltpu.VMEM((steps, pairs) + tile, BF16),
            pltpu.VMEM((pairs,) + tile, BF16),
            pltpu.VMEM((pairs,) + tile, F32),
            pltpu.VMEM((pairs,) + tile, F32),
            dma((own_blocks,)),
            dma,
            dma((steps, units, SUBS)),
            dma((steps, units, SUBS)),
            dma((outer, SUBS)),
            dma((outer, SUBS)),
            dma((units, SUBS)),
            dma((steps, outer, SUBS)),
            dma((steps, outer, SUBS)),
            dma((steps, 2, outer)),
            dma((steps, 2, outer)),
            dma((2, outer)),
            dma((2, outer)),
            dma((steps,)),
            dma,
        ],
        compiler_params=pltpu.CompilerParams(
            collective_id=0, has_side_effects=True, vmem_limit_bytes=60 * 2**20
        ),
        name="lstm",
    )(lay, perm, same, last, emb, weights[0].reshape(own_blocks, depth, gates), bias[0], d_hidden[0])

    whole = lambda shape: pl.BlockSpec(shape, lambda j: (0,) * len(shape))
    grad_w, grad_b, hidden = pl.pallas_call(
        weight_kernel,
        grid=(own_blocks,),
        out_shape=(
            jax.ShapeDtypeStruct((own_blocks, depth, gates), BF16),
            jax.ShapeDtypeStruct((own_blocks, gates), F32),
            jax.ShapeDtypeStruct((steps, rows, width), BF16),
        ),
        in_specs=[
            smem,
            whole((2 * half_blocks, block, steps * rows)),
            pl.BlockSpec((1, steps * rows, gates), lambda j: (j, 0, 0)),
            whole((steps, rows, width)),
        ],
        out_specs=(
            pl.BlockSpec((1, depth, gates), lambda j: (j, 0, 0)),
            whole((own_blocks, gates)),
            whole((steps, rows, width)),
        ),
        compiler_params=pltpu.CompilerParams(vmem_limit_bytes=32 * 2**20),
        name="grad_weights",
    )(lay, inputs_t, grad_pre, hidden)
    return (
        hidden[None],
        grad_w.reshape(1, own_blocks, nonzero, block, gates),
        grad_b[None],
    )


def solution(mesh):
    placed = (
        P(),
        P(None, "unit"),
        P("layer", "unit", None, None, None),
        P("layer", "unit", None),
        P("layer", "unit", None),
        P("layer", None, None, "unit"),
    )
    return jax.shard_map(
        functools.partial(on_device, mesh.shape["layer"], mesh.shape["unit"]),
        mesh=mesh,
        in_specs=placed,
        out_specs=(
            P("layer", None, None, "unit"),
            P("layer", "unit", None, None, None),
            P("layer", "unit", None),
        ),
        check_vma=False,
    )
```

```python
import functools

import jax
import jax.numpy as jnp
from jax import lax
from jax.experimental import pallas as pl
from jax.experimental.pallas import tpu as pltpu
from jax.sharding import PartitionSpec as P

MESH = pl.DeviceIdType.MESH
F32 = jnp.float32
BF16 = jnp.bfloat16
INNER = 2
SUBS = 2


def looped(count, unroll, body):
    while count % unroll:
        unroll -= 1

    def several(step, carry):
        for part in range(unroll):
            body(step * unroll + part)
        return carry

    lax.fori_loop(0, count // unroll, several, 0)


def lstm_kernel(
    layers,
    units,
    groups,
    lay_ref,
    perm_ref,
    same_ref,
    last_ref,
    emb_ref,
    w_hbm,
    bias_ref,
    cot_ref,
    hid_ref,
    xt_hbm,
    gp_ref,
    w_ref,
    wt_ref,
    xt_ref,
    x_ref,
    h_ref,
    s_ref,
    act_ref,
    cell_ref,
    c_ref,
    r_ref,
    p_ref,
    xr_ref,
    zr_ref,
    q_ref,
    d_ref,
    ds_ref,
    rec_ref,
    carry_ref,
    w_sem,
    xt_sem,
    h_recv,
    s_recv,
    z_send,
    x_send,
    up_send,
    ez_send,
    ex_send,
    xr_recv,
    zr_recv,
    xr_send,
    zr_send,
    d_recv,
    d_send,
):
    layer = lax.axis_index("layer")
    unit = lax.axis_index("unit")
    outer = units // INNER
    zpos = unit // INNER
    xpos = unit % INNER
    partner = zpos * INNER + (1 - xpos)
    steps, rows, _ = cot_ref.shape
    own_blocks, nonzero = lay_ref.shape
    pairs = own_blocks // 2
    sub_pairs = pairs // SUBS
    half_blocks = units * own_blocks
    entries = own_blocks * nonzero // groups
    has_above = layer < layers - 1
    has_below = layer > 0
    low = lax.broadcasted_iota(jnp.int32, (rows, 128), 1) < 64

    def other_z(dz):
        return lax.rem(zpos + dz, outer)

    def swap(tile):
        return pltpu.roll(tile, 64, axis=1)

    def remote(src, dst, send, recv, where_to):
        return pltpu.make_async_remote_copy(
            src_ref=src,
            dst_ref=dst,
            send_sem=send,
            recv_sem=recv,
            device_id=where_to,
            device_id_type=MESH,
        )

    barrier = pltpu.get_barrier_semaphore()

    def greet(where_to):
        pl.semaphore_signal(barrier, inc=1, device_id=where_to, device_id_type=MESH)

    for dz in range(1, outer):
        greet((layer, other_z(dz) * INNER + xpos))
    greet((layer, partner))

    @pl.when(has_above)
    def _():
        greet((layer + 1, unit))

    @pl.when(has_below)
    def _():
        greet((layer - 1, unit))

    pl.semaphore_wait(
        barrier, outer + lax.min(layers - 1 - layer, 1) + lax.min(layer, 1)
    )

    def part(ref, t, v, sub):
        return ref.at[t, v, pl.ds(sub * sub_pairs, sub_pairs)]

    def emb_z(t, dz, sub):
        here = part(s_ref, t, unit, sub)
        return remote(
            here,
            here,
            ez_send.at[t, dz, sub],
            s_recv.at[t, unit, sub],
            (layer, other_z(dz) * INNER + xpos),
        )

    def emb_x(t, dz, sub):
        v = other_z(dz) * INNER + xpos
        here = part(s_ref, t, v, sub)
        return remote(here, here, ex_send.at[t, dz, sub], s_recv.at[t, v, sub], (layer, partner))

    def s_wait(t, v, sub):
        here = part(s_ref, t, v, sub)
        remote(
            here, here, ex_send.at[t, 0, sub], s_recv.at[t, v, sub], (layer, partner)
        ).wait_recv()

    def emb_forward(t):
        for sub in range(SUBS):
            for dz in range(1, outer):
                s_wait(t, other_z(dz) * INNER + xpos, sub)
                emb_x(t, dz, sub).start()

    @pl.when(layer == 0)
    def _():
        for t in range(steps):
            s_ref[t, unit] = emb_ref[t]
            for sub in range(SUBS):
                for dz in range(1, outer):
                    emb_z(t, dz, sub).start()
                emb_x(t, 0, sub).start()

    def w_copy(j):
        return pltpu.make_async_copy(w_hbm.at[j], w_ref.at[j], w_sem.at[j])

    looped(own_blocks, 1, lambda j: w_copy(j).start())

    zero_tile = jnp.zeros((rows, 128), F32)

    def zero_x(b):
        x_ref[half_blocks + b] = jnp.zeros((rows, 128), BF16)

    looped(half_blocks, 8, zero_x)
    for q in range(pairs):
        rec_ref[q] = zero_tile
        carry_ref[q] = zero_tile
        cell_ref[0, q] = zero_tile
    for g in range(groups):
        r_ref[g * (entries + 1) + entries] = zero_tile.astype(BF16)

    @pl.when(layer == layers - 1)
    def _():
        for t in range(steps):
            for q in range(pairs):
                d_ref[t, q] = jnp.zeros((rows, 128), BF16)

    def unpack(src, t, v, base, sub):
        for part_q in range(sub_pairs):
            q = sub * sub_pairs + part_q
            tile = src[t, v, q].astype(F32)
            turned = swap(tile)
            at = base + v * own_blocks + 2 * q
            x_ref[at] = jnp.where(low, tile, turned).astype(BF16)
            x_ref[at + 1] = jnp.where(low, turned, tile).astype(BF16)

    @pl.when(layer == 0)
    def _():
        emb_forward(0)

    looped(own_blocks, 1, lambda j: w_copy(j).wait())

    def turn_weights():
        depth, gates = w_ref.shape[1:]

        def one(j):
            for at in range(0, depth, gates):
                wt_ref[j, :, at : at + gates] = w_ref[j, at : at + gates, :].T

        looped(own_blocks, 1, one)

    @pl.when(layer >= layers // 2)
    def _():
        turn_weights()

    def own_copy_z(t, dz, sub):
        here = part(h_ref, t, unit, sub)
        return remote(
            here,
            here,
            z_send.at[dz, sub],
            h_recv.at[t, unit, sub],
            (layer, other_z(dz) * INNER + xpos),
        )

    def copy_x(t, dz, sub):
        v = other_z(dz) * INNER + xpos
        here = part(h_ref, t, v, sub)
        return remote(here, here, x_send.at[dz, sub], h_recv.at[t, v, sub], (layer, partner))

    def copy_up(t, v, sub):
        return remote(
            part(h_ref, t, v, sub),
            part(s_ref, t, v, sub),
            up_send.at[v, sub],
            s_recv.at[t, v, sub],
            (layer + 1, unit),
        )

    def h_wait(t, v, sub):
        here = part(h_ref, t, v, sub)
        remote(
            here, here, x_send.at[0, sub], h_recv.at[t, v, sub], (layer, partner)
        ).wait_recv()

    def wait_up(t):
        @pl.when((layers - 1 - layer) * (t + 1) > 0)
        def _():
            def one(v):
                for sub in range(SUBS):
                    copy_up(t, v, sub).wait_send()

            looped(units, 1, one)

    def forward(t, carry):
        def take_source(i):
            v = lax.rem(unit + i, units)

            @pl.when(layer + lax.abs(lax.rem(v, INNER) - xpos) > 0)
            def _():
                for sub in range(SUBS):
                    s_wait(t, v, sub)

            for sub in range(SUBS):
                unpack(s_ref, t, v, 0, sub)

        looped(units, 1, take_source)

        def cells(q):
            pres = []
            for side in range(2):
                j = 2 * q + side
                tiles = []
                for k in range(0, nonzero, 2):
                    tiles.append(
                        jnp.where(low, x_ref[lay_ref[j, k]], x_ref[lay_ref[j, k + 1]])
                    )
                picked = jnp.concatenate(tiles, axis=1)
                pres.append(
                    jnp.dot(picked, w_ref[j], preferred_element_type=F32)
                    + bias_ref[pl.ds(j, 1), :]
                )
            first, second = pres
            i_pre = jnp.where(low, first[:, :128], swap(second[:, :128]))
            f_pre = jnp.where(low, swap(first[:, :128]), second[:, :128])
            u_pre = jnp.where(low, first[:, 128:], swap(second[:, 128:]))
            o_pre = jnp.where(low, swap(first[:, 128:]), second[:, 128:])
            in_gate = jax.nn.sigmoid(i_pre)
            forget = jax.nn.sigmoid(f_pre)
            update = jnp.tanh(u_pre)
            out_gate = jax.nn.sigmoid(o_pre)
            cell = forget * cell_ref[t, q] + in_gate * update
            squash = jnp.tanh(cell)
            hidden = (out_gate * squash).astype(BF16)
            cell_ref[t + 1, q] = cell
            act_ref[0, t, q] = in_gate
            act_ref[1, t, q] = forget
            act_ref[2, t, q] = update
            act_ref[3, t, q] = out_gate
            act_ref[4, t, q] = squash
            h_ref[t, unit, q] = hidden
            hid_ref[t, :, pl.ds(pl.multiple_of(q * 128, 128), 128)] = hidden

        wait_up(t - 1)
        for sub in range(SUBS):
            looped(sub_pairs, 2, lambda i: cells(sub * sub_pairs + i))

            @pl.when((layers - 1 - layer) + (steps - 1 - t) > 0)
            def _():
                for dz in range(1, outer):
                    own_copy_z(t, dz, sub).start()
                copy_x(t, 0, sub).start()

                @pl.when(has_above)
                def _():
                    copy_up(t, unit, sub).start()

        @pl.when((layers - 1 - layer) + (steps - 1 - t) > 0)
        def _():
            for sub in range(SUBS):
                unpack(h_ref, t, unit, half_blocks, sub)

            def arrived(dz, sub, is_partner):
                v = other_z(dz) * INNER + (1 - xpos if is_partner else xpos)
                h_wait(t, v, sub)
                if not is_partner:
                    copy_x(t, dz, sub).start()

                @pl.when(has_above)
                def _():
                    copy_up(t, v, sub).start()

                unpack(h_ref, t, v, half_blocks, sub)

            for sub in range(SUBS):
                looped(outer - 1, 1, lambda i: arrived(i + 1, sub, False))

            @pl.when(layer + lax.div(t + 1, steps) == 0)
            def _():
                emb_forward(t + 1)

            for sub in range(SUBS):
                looped(outer, 1, lambda i: arrived(i, sub, True))
            for sub in range(SUBS):
                for dz in range(1, outer):
                    own_copy_z(t, dz, sub).wait_send()
                for dz in range(outer):
                    copy_x(t, dz, sub).wait_send()

        return carry

    lax.fori_loop(0, steps, forward, 0)
    wait_up(steps - 1)

    xt_copy = pltpu.make_async_copy(xt_ref, xt_hbm, xt_sem)

    @pl.when(layer < layers // 2)
    def _():
        turn_weights()

    def turn_inputs():
        def one(at):
            v = at // pairs
            q = at % pairs
            source = jnp.concatenate([s_ref[t, v, q] for t in range(steps)], axis=0).T
            recur = jnp.concatenate(
                [jnp.zeros((rows, 128), BF16)] + [h_ref[t, v, q] for t in range(steps - 1)],
                axis=0,
            ).T
            for side in range(2):
                xt_ref[2 * at + side] = source[side * 64 : side * 64 + 64]
                xt_ref[half_blocks + 2 * at + side] = recur[side * 64 : side * 64 + 64]

        looped(units * pairs, 2, one)
        xt_copy.start()

    @pl.when(has_above)
    def _():
        turn_inputs()

    @pl.when(layer == 0)
    def _():
        for t in range(steps):
            for sub in range(SUBS):
                for dz in range(1, outer):
                    emb_z(t, dz, sub).wait_send()
                for dz in range(outer):
                    emb_x(t, dz, sub).wait_send()

    def group_sum(half, v, q):
        at = half * half_blocks + v * own_blocks + 2 * q
        total = None
        for g in range(groups):
            both = jnp.where(low, r_ref[last_ref[g, at]], r_ref[last_ref[g, at + 1]])
            both = both.astype(F32)
            total = both if total is None else total + both
        return total

    def copy_xr(t, half, z):
        return remote(
            p_ref.at[half, z],
            xr_ref.at[t, half, z],
            xr_send.at[half, z],
            xr_recv.at[t, half, z],
            (layer, partner),
        )

    def copy_zr(t, half, dz):
        z = other_z(dz)
        return remote(
            q_ref.at[half, z],
            zr_ref.at[t, half, zpos],
            zr_send.at[half, z],
            zr_recv.at[t, half, zpos],
            (layer, z * INNER + xpos),
        )

    def wait_zr(t, half, dz):
        z = other_z(dz)
        remote(
            q_ref.at[half, z],
            zr_ref.at[t, half, z],
            zr_send.at[half, z],
            zr_recv.at[t, half, z],
            (layer, z * INNER + xpos),
        ).wait_recv()

    def copy_down(t):
        return remote(ds_ref, d_ref.at[t], d_send, d_recv.at[t], (layer - 1, unit))

    def backward(i, carry):
        t = steps - 1 - i

        @pl.when(has_above)
        def _():
            remote(ds_ref, d_ref.at[t], d_send, d_recv.at[t], (layer + 1, unit)).wait_recv()

        def cells(q):
            grad_hidden = (
                cot_ref[t, :, pl.ds(pl.multiple_of(q * 128, 128), 128)].astype(F32)
                + d_ref[t, q].astype(F32)
                + rec_ref[q]
            )
            in_gate = act_ref[0, t, q]
            forget = act_ref[1, t, q]
            update = act_ref[2, t, q]
            out_gate = act_ref[3, t, q]
            squash = act_ref[4, t, q]
            grad_cell = carry_ref[q] + grad_hidden * out_gate * (1.0 - squash * squash)
            gi = grad_cell * update * in_gate * (1.0 - in_gate)
            gf = grad_cell * cell_ref[t, q] * forget * (1.0 - forget)
            gu = grad_cell * in_gate * (1.0 - update * update)
            go = grad_hidden * squash * out_gate * (1.0 - out_gate)
            carry_ref[q] = grad_cell * forget
            at = pl.ds(pl.multiple_of(t * rows, rows), rows)
            gp_ref[2 * q, at, :128] = jnp.where(low, gi, swap(gf)).astype(BF16)
            gp_ref[2 * q, at, 128:] = jnp.where(low, gu, swap(go)).astype(BF16)
            gp_ref[2 * q + 1, at, :128] = jnp.where(low, swap(gi), gf).astype(BF16)
            gp_ref[2 * q + 1, at, 128:] = jnp.where(low, swap(gu), go).astype(BF16)

        looped(pairs, 2, cells)

        @pl.when(layer + t > 0)
        def _():
            def contributions(j):
                grad_pre = gp_ref[j, pl.ds(pl.multiple_of(t * rows, rows), rows), :]
                contrib = jnp.dot(grad_pre, wt_ref[j], preferred_element_type=F32)
                for k in range(0, nonzero, 2):
                    tile = contrib[:, k * 64 : k * 64 + 128]
                    turned = swap(tile)
                    at = j * nonzero + k
                    c_ref[at] = jnp.where(low, tile, turned).astype(BF16)
                    c_ref[at + 1] = jnp.where(low, turned, tile).astype(BF16)

            looped(own_blocks, 2, contributions)

            def runs(r8, run):
                run = list(run)
                for part_r in range(8):
                    r = r8 * 8 + part_r
                    for g in range(groups):
                        keep = jnp.full((rows, 128), same_ref[g, r], F32).astype(BF16)
                        run[g] = c_ref[perm_ref[g, r]] + keep * run[g]
                        r_ref[g * (entries + 1) + r] = run[g]
                return tuple(run)

            zero_run = zero_tile.astype(BF16)
            lax.fori_loop(0, entries // 8, runs, (zero_run,) * groups)

            def per_half(do):
                @pl.when(t > 0)
                def _():
                    do(1)

                @pl.when(has_below)
                def _():
                    do(0)

            def send_partner(half):
                def one(i):
                    z = other_z(lax.rem(i + 1, outer))
                    for q in range(pairs):
                        p_ref[half, z, q] = group_sum(
                            half, z * INNER + (1 - xpos), q
                        ).astype(BF16)
                    copy_xr(t, half, z).start()

                looped(outer, 1, one)

            def send_along(half):
                def one(i):
                    dz = i + 1
                    z = other_z(dz)
                    copy_xr(t, half, z).wait_recv()
                    for q in range(pairs):
                        q_ref[half, z, q] = (
                            group_sum(half, z * INNER + xpos, q)
                            + xr_ref[t, half, z, q].astype(F32)
                        ).astype(BF16)
                    copy_zr(t, half, dz).start()

                looped(outer - 1, 1, one)

            def finish(half):
                copy_xr(t, half, zpos).wait_recv()
                for dz in range(1, outer):
                    wait_zr(t, half, dz)

                def one(q):
                    total = group_sum(half, unit, q) + xr_ref[t, half, zpos, q].astype(F32)
                    for dz in range(1, outer):
                        total = total + zr_ref[t, half, other_z(dz), q].astype(F32)
                    if half:
                        rec_ref[q] = total
                    else:
                        ds_ref[q] = total.astype(BF16)

                looped(pairs, 2, one)
                if not half:
                    copy_down(t).start()

            def settle(half):
                for z in range(outer):
                    copy_xr(t, half, z).wait_send()
                for dz in range(1, outer):
                    copy_zr(t, half, dz).wait_send()
                if not half:
                    copy_down(t).wait_send()

            per_half(send_partner)
            per_half(send_along)
            per_half(finish)
            per_half(settle)

        return carry

    lax.fori_loop(0, steps, backward, 0)

    @pl.when(layer == layers - 1)
    def _():
        turn_inputs()

    xt_copy.wait()


def weight_kernel(lay_ref, xt_ref, gp_ref, hid_ref, gw_ref, gb_ref, out_ref):
    j = pl.program_id(0)
    grad_pre = gp_ref[0]
    picked = jnp.concatenate(
        [xt_ref[lay_ref[j, k]] for k in range(lay_ref.shape[1])], axis=0
    )
    gw_ref[0] = jnp.dot(picked, grad_pre, preferred_element_type=F32).astype(BF16)
    gb_ref[pl.ds(j, 1), :] = jnp.sum(grad_pre.astype(F32), axis=0, keepdims=True)

    @pl.when(j == 0)
    def _():
        out_ref[...] = hid_ref[...]


def on_device(layers, units, tokens, embed, weights, layout, bias, d_hidden):
    steps, rows = tokens.shape
    vocab, width = embed.shape
    _, own_blocks, nonzero, block, gates = weights.shape
    pairs = own_blocks // 2
    half_blocks = units * own_blocks
    groups = 4 if own_blocks % 4 == 0 else 2
    entries = own_blocks * nonzero // groups
    outer = units // INNER
    depth = nonzero * block

    onehot = (tokens.reshape(-1)[:, None] == jnp.arange(vocab, dtype=jnp.int32)).astype(BF16)
    looked = jnp.dot(onehot, embed, preferred_element_type=F32).astype(BF16)
    emb = looked.reshape(steps, rows, pairs, 128).transpose(0, 2, 1, 3)

    lay = layout[0]
    ent = lay.reshape(groups, entries)
    spot = jnp.arange(entries, dtype=jnp.int32)
    key = ent * entries + spot
    rank = jnp.sum((key[:, None, :] < key[:, :, None]).astype(jnp.int32), -1)
    placed = rank[:, :, None] == spot
    perm = jnp.sum(jnp.where(placed, spot[:, None], 0), 1)
    ordered = jnp.sum(jnp.where(placed, ent[:, :, None], 0), 1)
    same = jnp.concatenate(
        [jnp.zeros((groups, 1), F32), (ordered[:, 1:] == ordered[:, :-1]).astype(F32)], 1
    )
    group_ids = jnp.arange(groups, dtype=jnp.int32)[:, None]
    perm = perm + group_ids * entries
    blocks = jnp.arange(2 * half_blocks, dtype=jnp.int32)[:, None]
    below = jnp.sum((ent[:, None, :] <= blocks).astype(jnp.int32), -1)
    present = jnp.any(ent[:, None, :] == blocks, -1)
    last = jnp.where(present, below - 1, entries) + group_ids * (entries + 1)

    smem = pl.BlockSpec(memory_space=pltpu.SMEM)
    vmem = pl.BlockSpec(memory_space=pltpu.VMEM)
    hbm = pl.BlockSpec(memory_space=pl.ANY)
    tile = (rows, 128)
    dma = pltpu.SemaphoreType.DMA
    hidden, inputs_t, grad_pre = pl.pallas_call(
        functools.partial(lstm_kernel, layers, units, groups),
        out_shape=(
            jax.ShapeDtypeStruct((steps, rows, width), BF16),
            jax.ShapeDtypeStruct((2 * half_blocks, block, steps * rows), BF16),
            jax.ShapeDtypeStruct((own_blocks, steps * rows, gates), BF16),
        ),
        in_specs=[smem, smem, smem, smem, vmem, hbm, vmem, vmem],
        out_specs=(vmem, hbm, vmem),
        scratch_shapes=[
            pltpu.VMEM((own_blocks, depth, gates), BF16),
            pltpu.VMEM((own_blocks, gates, depth), BF16),
            pltpu.VMEM((2 * half_blocks, block, steps * rows), BF16),
            pltpu.VMEM((2 * half_blocks,) + tile, BF16),
            pltpu.VMEM((steps, units, pairs) + tile, BF16),
            pltpu.VMEM((steps, units, pairs) + tile, BF16),
            pltpu.VMEM((5, steps, pairs) + tile, F32),
            pltpu.VMEM((steps + 1, pairs) + tile, F32),
            pltpu.VMEM((groups * entries,) + tile, BF16),
            pltpu.VMEM((groups * (entries + 1),) + tile, BF16),
            pltpu.VMEM((2, outer, pairs) + tile, BF16),
            pltpu.VMEM((steps, 2, outer, pairs) + tile, BF16),
            pltpu.VMEM((steps, 2, outer, pairs) + tile, BF16),
            pltpu.VMEM((2, outer, pairs) + tile, BF16),
            pltpu.VMEM((steps, pairs) + tile, BF16),
            pltpu.VMEM((pairs,) + tile, BF16),
            pltpu.VMEM((pairs,) + tile, F32),
            pltpu.VMEM((pairs,) + tile, F32),
            dma((own_blocks,)),
            dma,
            dma((steps, units, SUBS)),
            dma((steps, units, SUBS)),
            dma((outer, SUBS)),
            dma((outer, SUBS)),
            dma((units, SUBS)),
            dma((steps, outer, SUBS)),
            dma((steps, outer, SUBS)),
            dma((steps, 2, outer)),
            dma((steps, 2, outer)),
            dma((2, outer)),
            dma((2, outer)),
            dma((steps,)),
            dma,
        ],
        compiler_params=pltpu.CompilerParams(
            collective_id=0, has_side_effects=True, vmem_limit_bytes=62 * 2**20
        ),
        name="lstm",
    )(lay, perm, same, last, emb, weights[0].reshape(own_blocks, depth, gates), bias[0], d_hidden[0])

    whole = lambda shape: pl.BlockSpec(shape, lambda j: (0,) * len(shape))
    grad_w, grad_b, hidden = pl.pallas_call(
        weight_kernel,
        grid=(own_blocks,),
        out_shape=(
            jax.ShapeDtypeStruct((own_blocks, depth, gates), BF16),
            jax.ShapeDtypeStruct((own_blocks, gates), F32),
            jax.ShapeDtypeStruct((steps, rows, width), BF16),
        ),
        in_specs=[
            smem,
            whole((2 * half_blocks, block, steps * rows)),
            pl.BlockSpec((1, steps * rows, gates), lambda j: (j, 0, 0)),
            whole((steps, rows, width)),
        ],
        out_specs=(
            pl.BlockSpec((1, depth, gates), lambda j: (j, 0, 0)),
            whole((own_blocks, gates)),
            whole((steps, rows, width)),
        ),
        compiler_params=pltpu.CompilerParams(vmem_limit_bytes=32 * 2**20),
        name="grad_weights",
    )(lay, inputs_t, grad_pre, hidden)
    return (
        hidden[None],
        grad_w.reshape(1, own_blocks, nonzero, block, gates),
        grad_b[None],
    )


def solution(mesh):
    placed = (
        P(),
        P(None, "unit"),
        P("layer", "unit", None, None, None),
        P("layer", "unit", None),
        P("layer", "unit", None),
        P("layer", None, None, "unit"),
    )
    return jax.shard_map(
        functools.partial(on_device, mesh.shape["layer"], mesh.shape["unit"]),
        mesh=mesh,
        in_specs=placed,
        out_specs=(
            P("layer", None, None, "unit"),
            P("layer", "unit", None, None, None),
            P("layer", "unit", None),
        ),
        check_vma=False,
    )
```

```python
import functools

import jax
import jax.numpy as jnp
from jax import lax
from jax.experimental import pallas as pl
from jax.experimental.pallas import tpu as pltpu
from jax.sharding import PartitionSpec as P

MESH = pl.DeviceIdType.MESH
F32 = jnp.float32
BF16 = jnp.bfloat16
INNER = 2
SUBS = 2


def looped(count, unroll, body):
    while count % unroll:
        unroll -= 1

    def several(step, carry):
        for part in range(unroll):
            body(step * unroll + part)
        return carry

    lax.fori_loop(0, count // unroll, several, 0)


def lstm_kernel(
    layers,
    units,
    groups,
    lay_ref,
    perm_ref,
    same_ref,
    last_ref,
    emb_ref,
    w_hbm,
    bias_ref,
    cot_ref,
    hid_ref,
    xt_hbm,
    gp_ref,
    w_ref,
    wt_ref,
    xt_ref,
    x_ref,
    h_ref,
    s_ref,
    act_ref,
    cell_ref,
    c_ref,
    r_ref,
    p_ref,
    xr_ref,
    zr_ref,
    q_ref,
    d_ref,
    ds_ref,
    rec_ref,
    carry_ref,
    w_sem,
    xt_sem,
    h_recv,
    s_recv,
    z_send,
    x_send,
    up_send,
    ez_send,
    ex_send,
    xr_recv,
    zr_recv,
    xr_send,
    zr_send,
    d_recv,
    d_send,
):
    layer = lax.axis_index("layer")
    unit = lax.axis_index("unit")
    outer = units // INNER
    zpos = unit // INNER
    xpos = unit % INNER
    partner = zpos * INNER + (1 - xpos)
    steps, rows, _ = cot_ref.shape
    own_blocks, nonzero = lay_ref.shape
    pairs = own_blocks // 2
    sub_pairs = pairs // SUBS
    half_blocks = units * own_blocks
    entries = own_blocks * nonzero // groups
    has_above = layer < layers - 1
    has_below = layer > 0
    low = lax.broadcasted_iota(jnp.int32, (rows, 128), 1) < 64

    def other_z(dz):
        return lax.rem(zpos + dz, outer)

    def swap(tile):
        return pltpu.roll(tile, 64, axis=1)

    def remote(src, dst, send, recv, where_to):
        return pltpu.make_async_remote_copy(
            src_ref=src,
            dst_ref=dst,
            send_sem=send,
            recv_sem=recv,
            device_id=where_to,
            device_id_type=MESH,
        )

    barrier = pltpu.get_barrier_semaphore()

    def greet(where_to):
        pl.semaphore_signal(barrier, inc=1, device_id=where_to, device_id_type=MESH)

    for dz in range(1, outer):
        greet((layer, other_z(dz) * INNER + xpos))
    greet((layer, partner))

    @pl.when(has_above)
    def _():
        greet((layer + 1, unit))

    @pl.when(has_below)
    def _():
        greet((layer - 1, unit))

    pl.semaphore_wait(
        barrier, outer + lax.min(layers - 1 - layer, 1) + lax.min(layer, 1)
    )

    def part(ref, t, v, sub):
        return ref.at[t, v, pl.ds(sub * sub_pairs, sub_pairs)]

    def emb_z(t, dz, sub):
        here = part(s_ref, t, unit, sub)
        return remote(
            here,
            here,
            ez_send.at[t, dz, sub],
            s_recv.at[t, unit, sub],
            (layer, other_z(dz) * INNER + xpos),
        )

    def emb_x(t, dz, sub):
        v = other_z(dz) * INNER + xpos
        here = part(s_ref, t, v, sub)
        return remote(here, here, ex_send.at[t, dz, sub], s_recv.at[t, v, sub], (layer, partner))

    def s_wait(t, v, sub):
        here = part(s_ref, t, v, sub)
        remote(
            here, here, ex_send.at[t, 0, sub], s_recv.at[t, v, sub], (layer, partner)
        ).wait_recv()

    def emb_forward(t):
        for sub in range(SUBS):
            for dz in range(1, outer):
                s_wait(t, other_z(dz) * INNER + xpos, sub)
                emb_x(t, dz, sub).start()

    @pl.when(layer == 0)
    def _():
        for t in range(steps):
            s_ref[t, unit] = emb_ref[t]
            for sub in range(SUBS):
                for dz in range(1, outer):
                    emb_z(t, dz, sub).start()
                emb_x(t, 0, sub).start()

    def w_copy(j):
        return pltpu.make_async_copy(w_hbm.at[j], w_ref.at[j], w_sem.at[j])

    looped(own_blocks, 1, lambda j: w_copy(j).start())

    zero_tile = jnp.zeros((rows, 128), F32)

    def zero_x(b):
        x_ref[half_blocks + b] = jnp.zeros((rows, 128), BF16)

    looped(half_blocks, 8, zero_x)
    for q in range(pairs):
        rec_ref[q] = zero_tile
        carry_ref[q] = zero_tile
        cell_ref[0, q] = zero_tile
    for g in range(groups):
        r_ref[g * (entries + 1) + entries] = zero_tile.astype(BF16)

    @pl.when(layer == layers - 1)
    def _():
        for t in range(steps):
            for q in range(pairs):
                d_ref[t, q] = jnp.zeros((rows, 128), BF16)

    def unpack(src, t, v, base, sub):
        for part_q in range(sub_pairs):
            q = sub * sub_pairs + part_q
            tile = src[t, v, q].astype(F32)
            turned = swap(tile)
            at = base + v * own_blocks + 2 * q
            x_ref[at] = jnp.where(low, tile, turned).astype(BF16)
            x_ref[at + 1] = jnp.where(low, turned, tile).astype(BF16)

    @pl.when(layer == 0)
    def _():
        emb_forward(0)

    looped(own_blocks, 1, lambda j: w_copy(j).wait())

    def turn_weights():
        depth, gates = w_ref.shape[1:]

        def one(j):
            for at in range(0, depth, gates):
                wt_ref[j, :, at : at + gates] = w_ref[j, at : at + gates, :].T

        looped(own_blocks, 1, one)

    @pl.when(layer >= layers // 2)
    def _():
        turn_weights()

    def own_copy_z(t, dz, sub):
        here = part(h_ref, t, unit, sub)
        return remote(
            here,
            here,
            z_send.at[dz, sub],
            h_recv.at[t, unit, sub],
            (layer, other_z(dz) * INNER + xpos),
        )

    def copy_x(t, dz, sub):
        v = other_z(dz) * INNER + xpos
        here = part(h_ref, t, v, sub)
        return remote(here, here, x_send.at[dz, sub], h_recv.at[t, v, sub], (layer, partner))

    def copy_up(t, v, sub):
        return remote(
            part(h_ref, t, v, sub),
            part(s_ref, t, v, sub),
            up_send.at[v, sub],
            s_recv.at[t, v, sub],
            (layer + 1, unit),
        )

    def h_wait(t, v, sub):
        here = part(h_ref, t, v, sub)
        remote(
            here, here, x_send.at[0, sub], h_recv.at[t, v, sub], (layer, partner)
        ).wait_recv()

    def wait_up(t):
        @pl.when((layers - 1 - layer) * (t + 1) > 0)
        def _():
            def one(v):
                for sub in range(SUBS):
                    copy_up(t, v, sub).wait_send()

            looped(units, 1, one)

    def forward(t, carry):
        def take_source(i):
            v = lax.rem(unit + i, units)

            @pl.when(layer + lax.abs(lax.rem(v, INNER) - xpos) > 0)
            def _():
                for sub in range(SUBS):
                    s_wait(t, v, sub)

            for sub in range(SUBS):
                unpack(s_ref, t, v, 0, sub)

        looped(units, 1, take_source)

        def cells(q):
            pres = []
            for side in range(2):
                j = 2 * q + side
                tiles = []
                for k in range(0, nonzero, 2):
                    tiles.append(
                        jnp.where(low, x_ref[lay_ref[j, k]], x_ref[lay_ref[j, k + 1]])
                    )
                picked = jnp.concatenate(tiles, axis=1)
                pres.append(
                    jnp.dot(picked, w_ref[j], preferred_element_type=F32)
                    + bias_ref[pl.ds(j, 1), :]
                )
            first, second = pres
            i_pre = jnp.where(low, first[:, :128], swap(second[:, :128]))
            f_pre = jnp.where(low, swap(first[:, :128]), second[:, :128])
            u_pre = jnp.where(low, first[:, 128:], swap(second[:, 128:]))
            o_pre = jnp.where(low, swap(first[:, 128:]), second[:, 128:])
            in_gate = jax.nn.sigmoid(i_pre)
            forget = jax.nn.sigmoid(f_pre)
            update = jnp.tanh(u_pre)
            out_gate = jax.nn.sigmoid(o_pre)
            cell = forget * cell_ref[t, q] + in_gate * update
            squash = jnp.tanh(cell)
            hidden = (out_gate * squash).astype(BF16)
            cell_ref[t + 1, q] = cell
            act_ref[0, t, q] = in_gate
            act_ref[1, t, q] = forget
            act_ref[2, t, q] = update
            act_ref[3, t, q] = out_gate
            act_ref[4, t, q] = squash
            h_ref[t, unit, q] = hidden
            hid_ref[t, :, pl.ds(pl.multiple_of(q * 128, 128), 128)] = hidden

        wait_up(t - 1)
        for sub in range(SUBS):
            looped(sub_pairs, 2, lambda i: cells(sub * sub_pairs + i))

            @pl.when((layers - 1 - layer) + (steps - 1 - t) > 0)
            def _():
                for dz in range(1, outer):
                    own_copy_z(t, dz, sub).start()
                copy_x(t, 0, sub).start()

                @pl.when(has_above)
                def _():
                    copy_up(t, unit, sub).start()

        @pl.when((layers - 1 - layer) + (steps - 1 - t) > 0)
        def _():
            for sub in range(SUBS):
                unpack(h_ref, t, unit, half_blocks, sub)

            def arrived(dz, sub, is_partner):
                v = other_z(dz) * INNER + (1 - xpos if is_partner else xpos)
                h_wait(t, v, sub)
                if not is_partner:
                    copy_x(t, dz, sub).start()

                @pl.when(has_above)
                def _():
                    copy_up(t, v, sub).start()

                unpack(h_ref, t, v, half_blocks, sub)

            for sub in range(SUBS):
                looped(outer - 1, 1, lambda i: arrived(i + 1, sub, False))

            @pl.when(layer + lax.div(t + 1, steps) == 0)
            def _():
                emb_forward(t + 1)

            for sub in range(SUBS):
                looped(outer, 1, lambda i: arrived(i, sub, True))
            for sub in range(SUBS):
                for dz in range(1, outer):
                    own_copy_z(t, dz, sub).wait_send()
                for dz in range(outer):
                    copy_x(t, dz, sub).wait_send()

        return carry

    lax.fori_loop(0, steps, forward, 0)
    wait_up(steps - 1)

    xt_copy = pltpu.make_async_copy(xt_ref, xt_hbm, xt_sem)

    @pl.when(layer < layers // 2)
    def _():
        turn_weights()

    def turn_inputs():
        def one(at):
            v = at // pairs
            q = at % pairs
            source = jnp.concatenate([s_ref[t, v, q] for t in range(steps)], axis=0).T
            recur = jnp.concatenate(
                [jnp.zeros((rows, 128), BF16)] + [h_ref[t, v, q] for t in range(steps - 1)],
                axis=0,
            ).T
            for side in range(2):
                xt_ref[2 * at + side] = source[side * 64 : side * 64 + 64]
                xt_ref[half_blocks + 2 * at + side] = recur[side * 64 : side * 64 + 64]

        looped(units * pairs, 2, one)
        xt_copy.start()

    @pl.when(has_above)
    def _():
        turn_inputs()

    @pl.when(layer == 0)
    def _():
        for t in range(steps):
            for sub in range(SUBS):
                for dz in range(1, outer):
                    emb_z(t, dz, sub).wait_send()
                for dz in range(outer):
                    emb_x(t, dz, sub).wait_send()

    def group_sum(half, v, q):
        at = half * half_blocks + v * own_blocks + 2 * q
        total = None
        for g in range(groups):
            both = jnp.where(low, r_ref[last_ref[g, at]], r_ref[last_ref[g, at + 1]])
            both = both.astype(F32)
            total = both if total is None else total + both
        return total

    def cut(ref, *at):
        *front, sub = at
        return ref.at[(*front, pl.ds(sub * sub_pairs, sub_pairs))]

    def copy_xr(t, half, z, sub):
        return remote(
            cut(p_ref, half, z, sub),
            cut(xr_ref, t, half, z, sub),
            xr_send.at[half, z, sub],
            xr_recv.at[t, half, z, sub],
            (layer, partner),
        )

    def copy_zr(t, half, dz, sub):
        z = other_z(dz)
        return remote(
            cut(q_ref, half, z, sub),
            cut(zr_ref, t, half, zpos, sub),
            zr_send.at[half, z, sub],
            zr_recv.at[t, half, zpos, sub],
            (layer, z * INNER + xpos),
        )

    def wait_zr(t, half, dz, sub):
        z = other_z(dz)
        remote(
            cut(q_ref, half, z, sub),
            cut(zr_ref, t, half, z, sub),
            zr_send.at[half, z, sub],
            zr_recv.at[t, half, z, sub],
            (layer, z * INNER + xpos),
        ).wait_recv()

    def copy_down(t, sub, where_to):
        return remote(
            cut(ds_ref, sub), cut(d_ref, t, sub), d_send.at[sub], d_recv.at[t, sub], where_to
        )

    def finish(t, half, sub):
        copy_xr(t, half, zpos, sub).wait_recv()
        for dz in range(1, outer):
            wait_zr(t, half, dz, sub)

        def one(i):
            q = sub * sub_pairs + i
            total = group_sum(half, unit, q) + xr_ref[t, half, zpos, q].astype(F32)
            for dz in range(1, outer):
                total = total + zr_ref[t, half, other_z(dz), q].astype(F32)
            if half:
                rec_ref[q] = total
            else:
                ds_ref[q] = total.astype(BF16)

        looped(sub_pairs, 4, one)
        if not half:
            copy_down(t, sub, (layer - 1, unit)).start()

    def settle(t, half):
        for sub in range(SUBS):
            for z in range(outer):
                copy_xr(t, half, z, sub).wait_send()
            for dz in range(1, outer):
                copy_zr(t, half, dz, sub).wait_send()
            if not half:
                copy_down(t, sub, (layer - 1, unit)).wait_send()

    def backward(i, carry):
        t = steps - 1 - i

        def cells(q):
            grad_hidden = (
                cot_ref[t, :, pl.ds(pl.multiple_of(q * 128, 128), 128)].astype(F32)
                + d_ref[t, q].astype(F32)
                + rec_ref[q]
            )
            in_gate = act_ref[0, t, q]
            forget = act_ref[1, t, q]
            update = act_ref[2, t, q]
            out_gate = act_ref[3, t, q]
            squash = act_ref[4, t, q]
            grad_cell = carry_ref[q] + grad_hidden * out_gate * (1.0 - squash * squash)
            gi = grad_cell * update * in_gate * (1.0 - in_gate)
            gf = grad_cell * cell_ref[t, q] * forget * (1.0 - forget)
            gu = grad_cell * in_gate * (1.0 - update * update)
            go = grad_hidden * squash * out_gate * (1.0 - out_gate)
            carry_ref[q] = grad_cell * forget
            at = pl.ds(pl.multiple_of(t * rows, rows), rows)
            gp_ref[2 * q, at, :128] = jnp.where(low, gi, swap(gf)).astype(BF16)
            gp_ref[2 * q, at, 128:] = jnp.where(low, gu, swap(go)).astype(BF16)
            gp_ref[2 * q + 1, at, :128] = jnp.where(low, swap(gi), gf).astype(BF16)
            gp_ref[2 * q + 1, at, 128:] = jnp.where(low, swap(gu), go).astype(BF16)

        def contributions(j):
            grad_pre = gp_ref[j, pl.ds(pl.multiple_of(t * rows, rows), rows), :]
            contrib = jnp.dot(grad_pre, wt_ref[j], preferred_element_type=F32)
            for k in range(0, nonzero, 2):
                tile = contrib[:, k * 64 : k * 64 + 128]
                turned = swap(tile)
                at = j * nonzero + k
                c_ref[at] = jnp.where(low, tile, turned).astype(BF16)
                c_ref[at + 1] = jnp.where(low, turned, tile).astype(BF16)

        for sub in range(SUBS):

            @pl.when(i > 0)
            def _():
                finish(t + 1, 1, sub)

                @pl.when(has_below)
                def _():
                    finish(t + 1, 0, sub)

            @pl.when(has_above)
            def _():
                copy_down(t, sub, (layer + 1, unit)).wait_recv()

            looped(sub_pairs, 4, lambda part_q: cells(sub * sub_pairs + part_q))

            @pl.when(layer + t > 0)
            def _():
                looped(2 * sub_pairs, 2, lambda part_j: contributions(2 * sub * sub_pairs + part_j))

        @pl.when(i > 0)
        def _():
            settle(t + 1, 1)

            @pl.when(has_below)
            def _():
                settle(t + 1, 0)

        @pl.when(layer + t > 0)
        def _():
            def runs(r8, run):
                run = list(run)
                for part_r in range(8):
                    r = r8 * 8 + part_r
                    for g in range(groups):
                        keep = jnp.full((rows, 128), same_ref[g, r], F32).astype(BF16)
                        run[g] = c_ref[perm_ref[g, r]] + keep * run[g]
                        r_ref[g * (entries + 1) + r] = run[g]
                return tuple(run)

            zero_run = zero_tile.astype(BF16)
            lax.fori_loop(0, entries // 8, runs, (zero_run,) * groups)

            def per_half(do):
                @pl.when(t > 0)
                def _():
                    do(1)

                @pl.when(has_below)
                def _():
                    do(0)

            def send_partner(half, sub):
                def one(step):
                    z = other_z(lax.rem(step + 1, outer))
                    for part_q in range(sub_pairs):
                        q = sub * sub_pairs + part_q
                        p_ref[half, z, q] = group_sum(
                            half, z * INNER + (1 - xpos), q
                        ).astype(BF16)
                    copy_xr(t, half, z, sub).start()

                looped(outer, 1, one)

            def send_along(half, sub):
                def one(step):
                    dz = step + 1
                    z = other_z(dz)
                    copy_xr(t, half, z, sub).wait_recv()
                    for part_q in range(sub_pairs):
                        q = sub * sub_pairs + part_q
                        q_ref[half, z, q] = (
                            group_sum(half, z * INNER + xpos, q)
                            + xr_ref[t, half, z, q].astype(F32)
                        ).astype(BF16)
                    copy_zr(t, half, dz, sub).start()

                looped(outer - 1, 1, one)

            for sub in range(SUBS):
                per_half(lambda half: send_partner(half, sub))
            for sub in range(SUBS):
                per_half(lambda half: send_along(half, sub))

        return carry

    lax.fori_loop(0, steps, backward, 0)

    @pl.when(has_below)
    def _():
        for sub in range(SUBS):
            finish(0, 0, sub)
        settle(0, 0)

    @pl.when(layer == layers - 1)
    def _():
        turn_inputs()

    xt_copy.wait()


def weight_kernel(lay_ref, xt_ref, gp_ref, hid_ref, gw_ref, gb_ref, out_ref):
    step = pl.program_id(0)
    for part in range(gp_ref.shape[0]):
        j = step * gp_ref.shape[0] + part
        grad_pre = gp_ref[part]
        picked = jnp.concatenate(
            [xt_ref[lay_ref[j, k]] for k in range(lay_ref.shape[1])], axis=0
        )
        gw_ref[part] = jnp.dot(picked, grad_pre, preferred_element_type=F32).astype(BF16)
        gb_ref[pl.ds(j, 1), :] = jnp.sum(grad_pre.astype(F32), axis=0, keepdims=True)

    @pl.when(step == 0)
    def _():
        out_ref[...] = hid_ref[...]


def on_device(layers, units, tokens, embed, weights, layout, bias, d_hidden):
    steps, rows = tokens.shape
    vocab, width = embed.shape
    _, own_blocks, nonzero, block, gates = weights.shape
    pairs = own_blocks // 2
    half_blocks = units * own_blocks
    groups = 4 if own_blocks % 4 == 0 else 2
    entries = own_blocks * nonzero // groups
    outer = units // INNER
    depth = nonzero * block

    onehot = (tokens.reshape(-1)[:, None] == jnp.arange(vocab, dtype=jnp.int32)).astype(BF16)
    looked = jnp.dot(onehot, embed, preferred_element_type=F32).astype(BF16)
    emb = looked.reshape(steps, rows, pairs, 128).transpose(0, 2, 1, 3)

    lay = layout[0]
    ent = lay.reshape(groups, entries)
    spot = jnp.arange(entries, dtype=jnp.int32)
    key = ent * entries + spot
    rank = jnp.sum((key[:, None, :] < key[:, :, None]).astype(jnp.int32), -1)
    placed = rank[:, :, None] == spot
    perm = jnp.sum(jnp.where(placed, spot[:, None], 0), 1)
    ordered = jnp.sum(jnp.where(placed, ent[:, :, None], 0), 1)
    same = jnp.concatenate(
        [jnp.zeros((groups, 1), F32), (ordered[:, 1:] == ordered[:, :-1]).astype(F32)], 1
    )
    group_ids = jnp.arange(groups, dtype=jnp.int32)[:, None]
    perm = perm + group_ids * entries
    blocks = jnp.arange(2 * half_blocks, dtype=jnp.int32)[:, None]
    below = jnp.sum((ent[:, None, :] <= blocks).astype(jnp.int32), -1)
    present = jnp.any(ent[:, None, :] == blocks, -1)
    last = jnp.where(present, below - 1, entries) + group_ids * (entries + 1)

    smem = pl.BlockSpec(memory_space=pltpu.SMEM)
    vmem = pl.BlockSpec(memory_space=pltpu.VMEM)
    hbm = pl.BlockSpec(memory_space=pl.ANY)
    tile = (rows, 128)
    dma = pltpu.SemaphoreType.DMA
    hidden, inputs_t, grad_pre = pl.pallas_call(
        functools.partial(lstm_kernel, layers, units, groups),
        out_shape=(
            jax.ShapeDtypeStruct((steps, rows, width), BF16),
            jax.ShapeDtypeStruct((2 * half_blocks, block, steps * rows), BF16),
            jax.ShapeDtypeStruct((own_blocks, steps * rows, gates), BF16),
        ),
        in_specs=[smem, smem, smem, smem, vmem, hbm, vmem, vmem],
        out_specs=(vmem, hbm, vmem),
        scratch_shapes=[
            pltpu.VMEM((own_blocks, depth, gates), BF16),
            pltpu.VMEM((own_blocks, gates, depth), BF16),
            pltpu.VMEM((2 * half_blocks, block, steps * rows), BF16),
            pltpu.VMEM((2 * half_blocks,) + tile, BF16),
            pltpu.VMEM((steps, units, pairs) + tile, BF16),
            pltpu.VMEM((steps, units, pairs) + tile, BF16),
            pltpu.VMEM((5, steps, pairs) + tile, F32),
            pltpu.VMEM((steps + 1, pairs) + tile, F32),
            pltpu.VMEM((groups * entries,) + tile, BF16),
            pltpu.VMEM((groups * (entries + 1),) + tile, BF16),
            pltpu.VMEM((2, outer, pairs) + tile, BF16),
            pltpu.VMEM((steps, 2, outer, pairs) + tile, BF16),
            pltpu.VMEM((steps, 2, outer, pairs) + tile, BF16),
            pltpu.VMEM((2, outer, pairs) + tile, BF16),
            pltpu.VMEM((steps, pairs) + tile, BF16),
            pltpu.VMEM((pairs,) + tile, BF16),
            pltpu.VMEM((pairs,) + tile, F32),
            pltpu.VMEM((pairs,) + tile, F32),
            dma((own_blocks,)),
            dma,
            dma((steps, units, SUBS)),
            dma((steps, units, SUBS)),
            dma((outer, SUBS)),
            dma((outer, SUBS)),
            dma((units, SUBS)),
            dma((steps, outer, SUBS)),
            dma((steps, outer, SUBS)),
            dma((steps, 2, outer, SUBS)),
            dma((steps, 2, outer, SUBS)),
            dma((2, outer, SUBS)),
            dma((2, outer, SUBS)),
            dma((steps, SUBS)),
            dma((SUBS,)),
        ],
        compiler_params=pltpu.CompilerParams(
            collective_id=0, has_side_effects=True, vmem_limit_bytes=62 * 2**20
        ),
        name="lstm",
    )(lay, perm, same, last, emb, weights[0].reshape(own_blocks, depth, gates), bias[0], d_hidden[0])

    whole = lambda shape: pl.BlockSpec(shape, lambda j: (0,) * len(shape))
    grad_w, grad_b, hidden = pl.pallas_call(
        weight_kernel,
        grid=(own_blocks // 2,),
        out_shape=(
            jax.ShapeDtypeStruct((own_blocks, depth, gates), BF16),
            jax.ShapeDtypeStruct((own_blocks, gates), F32),
            jax.ShapeDtypeStruct((steps, rows, width), BF16),
        ),
        in_specs=[
            smem,
            whole((2 * half_blocks, block, steps * rows)),
            pl.BlockSpec((2, steps * rows, gates), lambda j: (j, 0, 0)),
            whole((steps, rows, width)),
        ],
        out_specs=(
            pl.BlockSpec((2, depth, gates), lambda j: (j, 0, 0)),
            whole((own_blocks, gates)),
            whole((steps, rows, width)),
        ),
        compiler_params=pltpu.CompilerParams(vmem_limit_bytes=32 * 2**20),
        name="grad_weights",
    )(lay, inputs_t, grad_pre, hidden)
    return (
        hidden[None],
        grad_w.reshape(1, own_blocks, nonzero, block, gates),
        grad_b[None],
    )


def solution(mesh):
    placed = (
        P(),
        P(None, "unit"),
        P("layer", "unit", None, None, None),
        P("layer", "unit", None),
        P("layer", "unit", None),
        P("layer", None, None, "unit"),
    )
    return jax.shard_map(
        functools.partial(on_device, mesh.shape["layer"], mesh.shape["unit"]),
        mesh=mesh,
        in_specs=placed,
        out_specs=(
            P("layer", None, None, "unit"),
            P("layer", "unit", None, None, None),
            P("layer", "unit", None),
        ),
        check_vma=False,
    )
```

```python
import functools

import jax
import jax.numpy as jnp
from jax import lax
from jax.experimental import pallas as pl
from jax.experimental.pallas import tpu as pltpu
from jax.sharding import PartitionSpec as P

MESH = pl.DeviceIdType.MESH
F32 = jnp.float32
BF16 = jnp.bfloat16
INNER = 2
SUBS = 2


def looped(count, unroll, body):
    while count % unroll:
        unroll -= 1

    def several(step, carry):
        for part in range(unroll):
            body(step * unroll + part)
        return carry

    lax.fori_loop(0, count // unroll, several, 0)


def lstm_kernel(
    layers,
    units,
    groups,
    lay_ref,
    perm_ref,
    same_ref,
    last_ref,
    emb_ref,
    w_hbm,
    bias_ref,
    cot_ref,
    hid_ref,
    xt_hbm,
    gp_ref,
    w_ref,
    wt_ref,
    xt_ref,
    x_ref,
    h_ref,
    s_ref,
    act_ref,
    cell_ref,
    c_ref,
    r_ref,
    p_ref,
    xr_ref,
    zr_ref,
    q_ref,
    d_ref,
    ds_ref,
    rec_ref,
    carry_ref,
    w_sem,
    xt_sem,
    h_recv,
    s_recv,
    z_send,
    x_send,
    up_send,
    ez_send,
    ex_send,
    xr_recv,
    zr_recv,
    xr_send,
    zr_send,
    d_recv,
    d_send,
):
    layer = lax.axis_index("layer")
    unit = lax.axis_index("unit")
    outer = units // INNER
    zpos = unit // INNER
    xpos = unit % INNER
    partner = zpos * INNER + (1 - xpos)
    steps, rows, _ = cot_ref.shape
    own_blocks, nonzero = lay_ref.shape
    pairs = own_blocks // 2
    sub_pairs = pairs // SUBS
    half_blocks = units * own_blocks
    entries = own_blocks * nonzero // groups
    has_above = layer < layers - 1
    has_below = layer > 0
    low = lax.broadcasted_iota(jnp.int32, (rows, 128), 1) < 64

    def other_z(dz):
        return lax.rem(zpos + dz, outer)

    def swap(tile):
        return pltpu.roll(tile, 64, axis=1)

    def remote(src, dst, send, recv, where_to):
        return pltpu.make_async_remote_copy(
            src_ref=src,
            dst_ref=dst,
            send_sem=send,
            recv_sem=recv,
            device_id=where_to,
            device_id_type=MESH,
        )

    barrier = pltpu.get_barrier_semaphore()

    def greet(where_to):
        pl.semaphore_signal(barrier, inc=1, device_id=where_to, device_id_type=MESH)

    for dz in range(1, outer):
        greet((layer, other_z(dz) * INNER + xpos))
    greet((layer, partner))

    @pl.when(has_above)
    def _():
        greet((layer + 1, unit))

    @pl.when(has_below)
    def _():
        greet((layer - 1, unit))

    pl.semaphore_wait(
        barrier, outer + lax.min(layers - 1 - layer, 1) + lax.min(layer, 1)
    )

    def part(ref, t, v, sub):
        return ref.at[t, v, pl.ds(sub * sub_pairs, sub_pairs)]

    def emb_z(t, dz, sub):
        here = part(s_ref, t, unit, sub)
        return remote(
            here,
            here,
            ez_send.at[t, dz, sub],
            s_recv.at[t, unit, sub],
            (layer, other_z(dz) * INNER + xpos),
        )

    def emb_x(t, dz, sub):
        v = other_z(dz) * INNER + xpos
        here = part(s_ref, t, v, sub)
        return remote(here, here, ex_send.at[t, dz, sub], s_recv.at[t, v, sub], (layer, partner))

    def s_wait(t, v, sub):
        here = part(s_ref, t, v, sub)
        remote(
            here, here, ex_send.at[t, 0, sub], s_recv.at[t, v, sub], (layer, partner)
        ).wait_recv()

    def emb_forward(t):
        for sub in range(SUBS):
            for dz in range(1, outer):
                s_wait(t, other_z(dz) * INNER + xpos, sub)
                emb_x(t, dz, sub).start()

    @pl.when(layer == 0)
    def _():
        for t in range(steps):
            s_ref[t, unit] = emb_ref[t]
            for sub in range(SUBS):
                for dz in range(1, outer):
                    emb_z(t, dz, sub).start()
                emb_x(t, 0, sub).start()

    def w_copy(j):
        return pltpu.make_async_copy(w_hbm.at[j], w_ref.at[j], w_sem.at[j])

    looped(own_blocks, 1, lambda j: w_copy(j).start())

    zero_tile = jnp.zeros((rows, 128), F32)

    def zero_x(b):
        x_ref[half_blocks + b] = jnp.zeros((rows, 128), BF16)

    looped(half_blocks, 8, zero_x)
    for q in range(pairs):
        rec_ref[q] = zero_tile
        carry_ref[q] = zero_tile
        cell_ref[0, q] = zero_tile
    for g in range(groups):
        r_ref[g * (entries + 1) + entries] = zero_tile.astype(BF16)

    @pl.when(layer == layers - 1)
    def _():
        for t in range(steps):
            for q in range(pairs):
                d_ref[t, q] = jnp.zeros((rows, 128), BF16)

    def unpack(src, t, v, base, sub):
        for part_q in range(sub_pairs):
            q = sub * sub_pairs + part_q
            tile = src[t, v, q].astype(F32)
            turned = swap(tile)
            at = base + v * own_blocks + 2 * q
            x_ref[at] = jnp.where(low, tile, turned).astype(BF16)
            x_ref[at + 1] = jnp.where(low, turned, tile).astype(BF16)

    @pl.when(layer == 0)
    def _():
        emb_forward(0)

    looped(own_blocks, 1, lambda j: w_copy(j).wait())

    def turn_weights():
        depth, gates = w_ref.shape[1:]

        def one(j):
            for at in range(0, depth, gates):
                wt_ref[j, :, at : at + gates] = w_ref[j, at : at + gates, :].T

        looped(own_blocks, 1, one)

    @pl.when(layer >= layers // 2)
    def _():
        turn_weights()

    def own_copy_z(t, dz, sub):
        here = part(h_ref, t, unit, sub)
        return remote(
            here,
            here,
            z_send.at[dz, sub],
            h_recv.at[t, unit, sub],
            (layer, other_z(dz) * INNER + xpos),
        )

    def copy_x(t, dz, sub):
        v = other_z(dz) * INNER + xpos
        here = part(h_ref, t, v, sub)
        return remote(here, here, x_send.at[dz, sub], h_recv.at[t, v, sub], (layer, partner))

    def copy_up(t, v, sub):
        return remote(
            part(h_ref, t, v, sub),
            part(s_ref, t, v, sub),
            up_send.at[v, sub],
            s_recv.at[t, v, sub],
            (layer + 1, unit),
        )

    def h_wait(t, v, sub):
        here = part(h_ref, t, v, sub)
        remote(
            here, here, x_send.at[0, sub], h_recv.at[t, v, sub], (layer, partner)
        ).wait_recv()

    def wait_up(t):
        @pl.when((layers - 1 - layer) * (t + 1) > 0)
        def _():
            def one(v):
                for sub in range(SUBS):
                    copy_up(t, v, sub).wait_send()

            looped(units, 1, one)

    def forward(t, carry):
        def take_source(i):
            v = lax.rem(unit + i, units)

            @pl.when(layer + lax.abs(lax.rem(v, INNER) - xpos) > 0)
            def _():
                for sub in range(SUBS):
                    s_wait(t, v, sub)

            for sub in range(SUBS):
                unpack(s_ref, t, v, 0, sub)

        looped(units, 1, take_source)

        def cells(q):
            pres = []
            for side in range(2):
                j = 2 * q + side
                tiles = []
                for k in range(0, nonzero, 2):
                    tiles.append(
                        jnp.where(low, x_ref[lay_ref[j, k]], x_ref[lay_ref[j, k + 1]])
                    )
                picked = jnp.concatenate(tiles, axis=1)
                pres.append(
                    jnp.dot(picked, w_ref[j], preferred_element_type=F32)
                    + bias_ref[pl.ds(j, 1), :]
                )
            first, second = pres
            i_pre = jnp.where(low, first[:, :128], swap(second[:, :128]))
            f_pre = jnp.where(low, swap(first[:, :128]), second[:, :128])
            u_pre = jnp.where(low, first[:, 128:], swap(second[:, 128:]))
            o_pre = jnp.where(low, swap(first[:, 128:]), second[:, 128:])
            in_gate = jax.nn.sigmoid(i_pre)
            forget = jax.nn.sigmoid(f_pre)
            update = jnp.tanh(u_pre)
            out_gate = jax.nn.sigmoid(o_pre)
            cell = forget * cell_ref[t, q] + in_gate * update
            squash = jnp.tanh(cell)
            hidden = (out_gate * squash).astype(BF16)
            cell_ref[t + 1, q] = cell
            act_ref[0, t, q] = in_gate
            act_ref[1, t, q] = forget
            act_ref[2, t, q] = update
            act_ref[3, t, q] = out_gate
            act_ref[4, t, q] = squash
            h_ref[t, unit, q] = hidden
            hid_ref[t, :, pl.ds(pl.multiple_of(q * 128, 128), 128)] = hidden

        wait_up(t - 1)
        for sub in range(SUBS):
            looped(sub_pairs, 4, lambda i: cells(sub * sub_pairs + i))

            @pl.when((layers - 1 - layer) + (steps - 1 - t) > 0)
            def _():
                for dz in range(1, outer):
                    own_copy_z(t, dz, sub).start()
                copy_x(t, 0, sub).start()

                @pl.when(has_above)
                def _():
                    copy_up(t, unit, sub).start()

        @pl.when((layers - 1 - layer) + (steps - 1 - t) > 0)
        def _():
            for sub in range(SUBS):
                unpack(h_ref, t, unit, half_blocks, sub)

            def arrived(dz, sub, is_partner):
                v = other_z(dz) * INNER + (1 - xpos if is_partner else xpos)
                h_wait(t, v, sub)
                if not is_partner:
                    copy_x(t, dz, sub).start()

                @pl.when(has_above)
                def _():
                    copy_up(t, v, sub).start()

                unpack(h_ref, t, v, half_blocks, sub)

            for sub in range(SUBS):
                looped(outer - 1, 1, lambda i: arrived(i + 1, sub, False))

            @pl.when(layer + lax.div(t + 1, steps) == 0)
            def _():
                emb_forward(t + 1)

            for sub in range(SUBS):
                looped(outer, 1, lambda i: arrived(i, sub, True))
            for sub in range(SUBS):
                for dz in range(1, outer):
                    own_copy_z(t, dz, sub).wait_send()
                for dz in range(outer):
                    copy_x(t, dz, sub).wait_send()

        return carry

    lax.fori_loop(0, steps, forward, 0)
    wait_up(steps - 1)

    xt_copy = pltpu.make_async_copy(xt_ref, xt_hbm, xt_sem)

    @pl.when(layer < layers // 2)
    def _():
        turn_weights()

    def turn_inputs():
        def one(at):
            v = at // pairs
            q = at % pairs
            source = jnp.concatenate([s_ref[t, v, q] for t in range(steps)], axis=0).T
            recur = jnp.concatenate(
                [jnp.zeros((rows, 128), BF16)] + [h_ref[t, v, q] for t in range(steps - 1)],
                axis=0,
            ).T
            for side in range(2):
                xt_ref[2 * at + side] = source[side * 64 : side * 64 + 64]
                xt_ref[half_blocks + 2 * at + side] = recur[side * 64 : side * 64 + 64]

        looped(units * pairs, 2, one)
        xt_copy.start()

    @pl.when(has_above)
    def _():
        turn_inputs()

    @pl.when(layer == 0)
    def _():
        for t in range(steps):
            for sub in range(SUBS):
                for dz in range(1, outer):
                    emb_z(t, dz, sub).wait_send()
                for dz in range(outer):
                    emb_x(t, dz, sub).wait_send()

    def group_sum(half, v, q):
        at = half * half_blocks + v * own_blocks + 2 * q
        total = None
        for g in range(groups):
            both = jnp.where(low, r_ref[last_ref[g, at]], r_ref[last_ref[g, at + 1]])
            both = both.astype(F32)
            total = both if total is None else total + both
        return total

    def cut(ref, *at):
        *front, sub = at
        return ref.at[(*front, pl.ds(sub * sub_pairs, sub_pairs))]

    def copy_xr(t, half, z, sub):
        return remote(
            cut(p_ref, half, z, sub),
            cut(xr_ref, t, half, z, sub),
            xr_send.at[half, z, sub],
            xr_recv.at[t, half, z, sub],
            (layer, partner),
        )

    def copy_zr(t, half, dz, sub):
        z = other_z(dz)
        return remote(
            cut(q_ref, half, z, sub),
            cut(zr_ref, t, half, zpos, sub),
            zr_send.at[half, z, sub],
            zr_recv.at[t, half, zpos, sub],
            (layer, z * INNER + xpos),
        )

    def wait_zr(t, half, dz, sub):
        z = other_z(dz)
        remote(
            cut(q_ref, half, z, sub),
            cut(zr_ref, t, half, z, sub),
            zr_send.at[half, z, sub],
            zr_recv.at[t, half, z, sub],
            (layer, z * INNER + xpos),
        ).wait_recv()

    def copy_down(t, sub, where_to):
        return remote(
            cut(ds_ref, sub), cut(d_ref, t, sub), d_send.at[sub], d_recv.at[t, sub], where_to
        )

    def finish(t, half, sub):
        copy_xr(t, half, zpos, sub).wait_recv()
        for dz in range(1, outer):
            wait_zr(t, half, dz, sub)

        def one(i):
            q = sub * sub_pairs + i
            total = group_sum(half, unit, q) + xr_ref[t, half, zpos, q].astype(F32)
            for dz in range(1, outer):
                total = total + zr_ref[t, half, other_z(dz), q].astype(F32)
            if half:
                rec_ref[q] = total
            else:
                ds_ref[q] = total.astype(BF16)

        looped(sub_pairs, 4, one)
        if not half:
            copy_down(t, sub, (layer - 1, unit)).start()

    def settle(t, half):
        for sub in range(SUBS):
            for z in range(outer):
                copy_xr(t, half, z, sub).wait_send()
            for dz in range(1, outer):
                copy_zr(t, half, dz, sub).wait_send()
            if not half:
                copy_down(t, sub, (layer - 1, unit)).wait_send()

    def backward(i, carry):
        t = steps - 1 - i

        def cells(q):
            grad_hidden = (
                cot_ref[t, :, pl.ds(pl.multiple_of(q * 128, 128), 128)].astype(F32)
                + d_ref[t, q].astype(F32)
                + rec_ref[q]
            )
            in_gate = act_ref[0, t, q]
            forget = act_ref[1, t, q]
            update = act_ref[2, t, q]
            out_gate = act_ref[3, t, q]
            squash = act_ref[4, t, q]
            grad_cell = carry_ref[q] + grad_hidden * out_gate * (1.0 - squash * squash)
            gi = grad_cell * update * in_gate * (1.0 - in_gate)
            gf = grad_cell * cell_ref[t, q] * forget * (1.0 - forget)
            gu = grad_cell * in_gate * (1.0 - update * update)
            go = grad_hidden * squash * out_gate * (1.0 - out_gate)
            carry_ref[q] = grad_cell * forget
            at = pl.ds(pl.multiple_of(t * rows, rows), rows)
            gp_ref[2 * q, at, :128] = jnp.where(low, gi, swap(gf)).astype(BF16)
            gp_ref[2 * q, at, 128:] = jnp.where(low, gu, swap(go)).astype(BF16)
            gp_ref[2 * q + 1, at, :128] = jnp.where(low, swap(gi), gf).astype(BF16)
            gp_ref[2 * q + 1, at, 128:] = jnp.where(low, swap(gu), go).astype(BF16)

        def contributions(j):
            grad_pre = gp_ref[j, pl.ds(pl.multiple_of(t * rows, rows), rows), :]
            contrib = jnp.dot(grad_pre, wt_ref[j], preferred_element_type=F32)
            for k in range(0, nonzero, 2):
                tile = contrib[:, k * 64 : k * 64 + 128]
                turned = swap(tile)
                at = j * nonzero + k
                c_ref[at] = jnp.where(low, tile, turned).astype(BF16)
                c_ref[at + 1] = jnp.where(low, turned, tile).astype(BF16)

        for sub in range(SUBS):

            @pl.when(i > 0)
            def _():
                finish(t + 1, 1, sub)

                @pl.when(has_below)
                def _():
                    finish(t + 1, 0, sub)

            @pl.when(has_above)
            def _():
                copy_down(t, sub, (layer + 1, unit)).wait_recv()

            looped(sub_pairs, 4, lambda part_q: cells(sub * sub_pairs + part_q))

            @pl.when(layer + t > 0)
            def _():
                looped(2 * sub_pairs, 4, lambda part_j: contributions(2 * sub * sub_pairs + part_j))

        @pl.when(i > 0)
        def _():
            settle(t + 1, 1)

            @pl.when(has_below)
            def _():
                settle(t + 1, 0)

        @pl.when(layer + t > 0)
        def _():
            def runs(r8, run):
                run = list(run)
                for part_r in range(8):
                    r = r8 * 8 + part_r
                    for g in range(groups):
                        keep = jnp.full((rows, 128), same_ref[g, r], F32).astype(BF16)
                        run[g] = c_ref[perm_ref[g, r]] + keep * run[g]
                        r_ref[g * (entries + 1) + r] = run[g]
                return tuple(run)

            zero_run = zero_tile.astype(BF16)
            lax.fori_loop(0, entries // 8, runs, (zero_run,) * groups)

            def per_half(do):
                @pl.when(t > 0)
                def _():
                    do(1)

                @pl.when(has_below)
                def _():
                    do(0)

            def send_partner(half, sub):
                def one(step):
                    z = other_z(lax.rem(step + 1, outer))
                    for part_q in range(sub_pairs):
                        q = sub * sub_pairs + part_q
                        p_ref[half, z, q] = group_sum(
                            half, z * INNER + (1 - xpos), q
                        ).astype(BF16)
                    copy_xr(t, half, z, sub).start()

                looped(outer, 1, one)

            def send_along(half, sub):
                def one(step):
                    dz = step + 1
                    z = other_z(dz)
                    copy_xr(t, half, z, sub).wait_recv()
                    for part_q in range(sub_pairs):
                        q = sub * sub_pairs + part_q
                        q_ref[half, z, q] = (
                            group_sum(half, z * INNER + xpos, q)
                            + xr_ref[t, half, z, q].astype(F32)
                        ).astype(BF16)
                    copy_zr(t, half, dz, sub).start()

                looped(outer - 1, 1, one)

            for sub in range(SUBS):
                per_half(lambda half: send_partner(half, sub))
            for sub in range(SUBS):
                per_half(lambda half: send_along(half, sub))

        return carry

    lax.fori_loop(0, steps, backward, 0)

    @pl.when(has_below)
    def _():
        for sub in range(SUBS):
            finish(0, 0, sub)
        settle(0, 0)

    @pl.when(layer == layers - 1)
    def _():
        turn_inputs()

    xt_copy.wait()


def weight_kernel(lay_ref, xt_ref, gp_ref, hid_ref, gw_ref, gb_ref, out_ref):
    step = pl.program_id(0)
    for part in range(gp_ref.shape[0]):
        j = step * gp_ref.shape[0] + part
        grad_pre = gp_ref[part]
        picked = jnp.concatenate(
            [xt_ref[lay_ref[j, k]] for k in range(lay_ref.shape[1])], axis=0
        )
        gw_ref[part] = jnp.dot(picked, grad_pre, preferred_element_type=F32).astype(BF16)
        gb_ref[pl.ds(j, 1), :] = jnp.sum(grad_pre.astype(F32), axis=0, keepdims=True)

    @pl.when(step == 0)
    def _():
        out_ref[...] = hid_ref[...]


def on_device(layers, units, tokens, embed, weights, layout, bias, d_hidden):
    steps, rows = tokens.shape
    vocab, width = embed.shape
    _, own_blocks, nonzero, block, gates = weights.shape
    pairs = own_blocks // 2
    half_blocks = units * own_blocks
    groups = 4 if own_blocks % 4 == 0 else 2
    entries = own_blocks * nonzero // groups
    outer = units // INNER
    depth = nonzero * block

    onehot = (tokens.reshape(-1)[:, None] == jnp.arange(vocab, dtype=jnp.int32)).astype(BF16)
    looked = jnp.dot(onehot, embed, preferred_element_type=F32).astype(BF16)
    emb = looked.reshape(steps, rows, pairs, 128).transpose(0, 2, 1, 3)

    lay = layout[0]
    ent = lay.reshape(groups, entries)
    spot = jnp.arange(entries, dtype=jnp.int32)
    key = ent * entries + spot
    rank = jnp.sum((key[:, None, :] < key[:, :, None]).astype(jnp.int32), -1)
    placed = rank[:, :, None] == spot
    perm = jnp.sum(jnp.where(placed, spot[:, None], 0), 1)
    ordered = jnp.sum(jnp.where(placed, ent[:, :, None], 0), 1)
    same = jnp.concatenate(
        [jnp.zeros((groups, 1), F32), (ordered[:, 1:] == ordered[:, :-1]).astype(F32)], 1
    )
    group_ids = jnp.arange(groups, dtype=jnp.int32)[:, None]
    perm = perm + group_ids * entries
    blocks = jnp.arange(2 * half_blocks, dtype=jnp.int32)[:, None]
    below = jnp.sum((ent[:, None, :] <= blocks).astype(jnp.int32), -1)
    present = jnp.any(ent[:, None, :] == blocks, -1)
    last = jnp.where(present, below - 1, entries) + group_ids * (entries + 1)

    smem = pl.BlockSpec(memory_space=pltpu.SMEM)
    vmem = pl.BlockSpec(memory_space=pltpu.VMEM)
    hbm = pl.BlockSpec(memory_space=pl.ANY)
    tile = (rows, 128)
    dma = pltpu.SemaphoreType.DMA
    hidden, inputs_t, grad_pre = pl.pallas_call(
        functools.partial(lstm_kernel, layers, units, groups),
        out_shape=(
            jax.ShapeDtypeStruct((steps, rows, width), BF16),
            jax.ShapeDtypeStruct((2 * half_blocks, block, steps * rows), BF16),
            jax.ShapeDtypeStruct((own_blocks, steps * rows, gates), BF16),
        ),
        in_specs=[smem, smem, smem, smem, vmem, hbm, vmem, vmem],
        out_specs=(vmem, hbm, vmem),
        scratch_shapes=[
            pltpu.VMEM((own_blocks, depth, gates), BF16),
            pltpu.VMEM((own_blocks, gates, depth), BF16),
            pltpu.VMEM((2 * half_blocks, block, steps * rows), BF16),
            pltpu.VMEM((2 * half_blocks,) + tile, BF16),
            pltpu.VMEM((steps, units, pairs) + tile, BF16),
            pltpu.VMEM((steps, units, pairs) + tile, BF16),
            pltpu.VMEM((5, steps, pairs) + tile, F32),
            pltpu.VMEM((steps + 1, pairs) + tile, F32),
            pltpu.VMEM((groups * entries,) + tile, BF16),
            pltpu.VMEM((groups * (entries + 1),) + tile, BF16),
            pltpu.VMEM((2, outer, pairs) + tile, BF16),
            pltpu.VMEM((steps, 2, outer, pairs) + tile, BF16),
            pltpu.VMEM((steps, 2, outer, pairs) + tile, BF16),
            pltpu.VMEM((2, outer, pairs) + tile, BF16),
            pltpu.VMEM((steps, pairs) + tile, BF16),
            pltpu.VMEM((pairs,) + tile, BF16),
            pltpu.VMEM((pairs,) + tile, F32),
            pltpu.VMEM((pairs,) + tile, F32),
            dma((own_blocks,)),
            dma,
            dma((steps, units, SUBS)),
            dma((steps, units, SUBS)),
            dma((outer, SUBS)),
            dma((outer, SUBS)),
            dma((units, SUBS)),
            dma((steps, outer, SUBS)),
            dma((steps, outer, SUBS)),
            dma((steps, 2, outer, SUBS)),
            dma((steps, 2, outer, SUBS)),
            dma((2, outer, SUBS)),
            dma((2, outer, SUBS)),
            dma((steps, SUBS)),
            dma((SUBS,)),
        ],
        compiler_params=pltpu.CompilerParams(
            collective_id=0, has_side_effects=True, vmem_limit_bytes=62 * 2**20
        ),
        name="lstm",
    )(lay, perm, same, last, emb, weights[0].reshape(own_blocks, depth, gates), bias[0], d_hidden[0])

    whole = lambda shape: pl.BlockSpec(shape, lambda j: (0,) * len(shape))
    grad_w, grad_b, hidden = pl.pallas_call(
        weight_kernel,
        grid=(own_blocks // 2,),
        out_shape=(
            jax.ShapeDtypeStruct((own_blocks, depth, gates), BF16),
            jax.ShapeDtypeStruct((own_blocks, gates), F32),
            jax.ShapeDtypeStruct((steps, rows, width), BF16),
        ),
        in_specs=[
            smem,
            whole((2 * half_blocks, block, steps * rows)),
            pl.BlockSpec((2, steps * rows, gates), lambda j: (j, 0, 0)),
            whole((steps, rows, width)),
        ],
        out_specs=(
            pl.BlockSpec((2, depth, gates), lambda j: (j, 0, 0)),
            whole((own_blocks, gates)),
            whole((steps, rows, width)),
        ),
        compiler_params=pltpu.CompilerParams(vmem_limit_bytes=62 * 2**20),
        name="grad_weights",
    )(lay, inputs_t, grad_pre, hidden)
    return (
        hidden[None],
        grad_w.reshape(1, own_blocks, nonzero, block, gates),
        grad_b[None],
    )


def solution(mesh):
    placed = (
        P(),
        P(None, "unit"),
        P("layer", "unit", None, None, None),
        P("layer", "unit", None),
        P("layer", "unit", None),
        P("layer", None, None, "unit"),
    )
    return jax.shard_map(
        functools.partial(on_device, mesh.shape["layer"], mesh.shape["unit"]),
        mesh=mesh,
        in_specs=placed,
        out_specs=(
            P("layer", None, None, "unit"),
            P("layer", "unit", None, None, None),
            P("layer", "unit", None),
        ),
        check_vma=False,
    )
```
